128 devices in a mesh: expert: 8 (over z, x_hi), tensor: 16 (over y, x_lo, core).
Axes of the slice: x: 4 (x_hi: 2, x_lo: 2; x = x_hi * 2 + x_lo), y: 4, z: 4, core: 2. Of those that a mesh axis runs over, the one named last changes fastest.
Arguments:
- tokens: bfloat16 [8, 1024, 3072], P('expert', 'tensor'), may hold values from -18 to 18
- expert_ids: int32 [8, 1024, 2], P('expert', 'tensor'), may hold values from 0 to 7, as said below
- slot_ids: int32 [8, 1024, 2], P('expert', 'tensor'), may hold values from 0 to 23, as said below
- norm_attn: bfloat16 [3072], replicated, may hold values from 0.099609375 to 1.8984375
- w_qkv: bfloat16 [3072, 3, 4096], P(None, None, 'tensor'), may hold values from -2 to 2
- w_out: bfloat16 [4096, 3072], P('tensor'), may hold values from -0.5 to 0.5
- norm_moe: bfloat16 [3072], replicated, may hold values from 0.099609375 to 1.8984375
- router_weight: bfloat16 [3072, 8], replicated, may hold values from -0.02734375 to 0.02734375
- w_gate_up: bfloat16 [8, 3072, 2, 12288], P('expert', None, None, 'tensor'), may hold values from -0.109375 to 0.109375
- w_down: bfloat16 [8, 12288, 3072], P('expert', 'tensor'), may hold values from -0.21875 to 0.21875
Outputs:
- layer_out: bfloat16 [8, 1024, 3072], P('expert', 'tensor')
The draws below stay inside these ranges and needn't reach their ends.
Inputs may be any that keep to these rules, and one draw needn't show every extreme that they name: `expert_ids`: each token names two different experts. Among the 64 tokens of one block no expert is named more than 24 times, and one and the same expert is named exactly 24 times in every block. `slot_ids`: A token's slot at an expert is the number of earlier tokens of its block that name the same expert.
All inputs are finite; a program needn't handle non-finite values.
Results may differ from the reference program's by a relative error of at most 0.025.
Values may be sent and summed in bfloat16 or wider, within the bound.
No kernel may reach another device: no remote copies, remote signals or barrier semaphores. Data moves between devices by JAX's collectives and lax.ppermute only.
A program may use at most 192 MiB of HBM per device.

```python
import jax
import jax.numpy as jnp
from jax import lax

D = 3072
HEADS = 32
HD = 128
FFE = 12288
TOK_DEV = 64
EXPERTS = 8
SEQS = 8
LEN = 1024
MOST = 24
CAP = 12


def route_plan(key):
    blocks = SEQS * LEN // TOK_DEV
    key_hot, key_rank, key_offset, key_label, key_side = jax.random.split(key, 5)
    hot = jax.random.randint(key_hot, (), 0, EXPERTS)
    ranks = jax.vmap(lambda item: jax.random.permutation(item, TOK_DEV))(jax.random.split(key_rank, blocks)).astype(jnp.int32)
    others = EXPERTS - 1
    offsets = jax.random.randint(key_offset, (blocks, 1), 0, others)
    relabel = jax.vmap(lambda item: jax.random.permutation(item, others))(jax.random.split(key_label, blocks)).astype(jnp.int32)
    is_hot = ranks < MOST
    position = jnp.where(is_hot, ranks, MOST + 2 * (ranks - MOST))
    label_one = jnp.take_along_axis(relabel, (offsets + position) % others, axis=1)
    label_two = jnp.take_along_axis(relabel, (offsets + position + 1) % others, axis=1)
    expert_one = label_one + (label_one >= hot).astype(jnp.int32)
    expert_two = label_two + (label_two >= hot).astype(jnp.int32)
    main_pick = jnp.where(is_hot, hot, expert_two)
    swap_side = jax.random.randint(key_side, (blocks, TOK_DEV), 0, 2) == 1
    column_a = jnp.where(swap_side, expert_one, main_pick)
    column_b = jnp.where(swap_side, main_pick, expert_one)
    chosen = jnp.stack([column_a, column_b], axis=-1).astype(jnp.int32)
    labels = jnp.arange(EXPERTS, dtype=jnp.int32)
    named = jnp.sum((chosen[..., None] == labels).astype(jnp.int32), axis=2)
    before = jnp.cumsum(named, axis=1) - named
    slots = jnp.take_along_axis(before, chosen, axis=2).astype(jnp.int32)
    return (chosen.reshape(SEQS, LEN, 2), slots.reshape(SEQS, LEN, 2))


def draw_expert_ids(key, part):
    return route_plan(key)[0]


def draw_slot_ids(key, part):
    return route_plan(key)[1]


def draw_tokens(key, part):
    key = jax.random.fold_in(key, 11)
    key_base = jax.random.fold_in(key, 0)
    values = jax.random.truncated_normal(key_base, -6.0, 6.0, (SEQS, LEN, D), jnp.float32)
    return values.astype(jnp.bfloat16)


def draw_w_qkv(key, part):
    key = jax.random.fold_in(key, 23)
    key_query, key_key, key_value = jax.random.split(key, 3)
    spread = D ** (-0.5)
    shape_one = (D, 1, HEADS, HD)
    query_part = jax.random.truncated_normal(key_query, -4.0, 4.0, shape_one, jnp.float32) * spread
    key_part = jax.random.truncated_normal(key_key, -4.0, 4.0, shape_one, jnp.float32) * spread
    value_part = jax.random.truncated_normal(key_value, -4.0, 4.0, shape_one, jnp.float32) * spread
    stacked = jnp.concatenate([query_part, key_part, value_part], axis=1)
    return stacked.reshape(D, 3, HEADS * HD).astype(jnp.bfloat16)


def block_scale(stream_key, dims, shards, low, top_value):
    def one(dim, shards_of):
        draws = jax.random.uniform(jax.random.fold_in(jax.random.fold_in(stream_key, 6), dim), (shards_of,), jnp.float32, low / len(shards), top_value / len(shards))
        return jnp.repeat(jnp.exp(draws), dims[dim] // shards_of).reshape((-1,) + (1,) * (len(dims) - dim - 1))

    loudness = one(*shards[0])
    for cut in shards[1:]:
        loudness = loudness * one(*cut)
    return loudness


def scatter_about(stream_key, dims, width, limit, cuts=(), kind=jnp.bfloat16):
    loudness = block_scale(stream_key, dims, cuts, -0.22, 0.18) if cuts else 1.0
    values = jax.random.normal(stream_key, dims, jnp.float32) * width * loudness
    return jnp.minimum(jnp.maximum(values, -limit), limit).astype(kind)


def setup_inputs(seed: int = 0) -> dict:
    key_of = jax.random.split(jax.random.key(seed), 11)
    tokens = draw_tokens(jax.random.fold_in(key_of[10], 71), 0)
    expert_ids = draw_expert_ids(jax.random.fold_in(key_of[10], 71), 0)
    slot_ids = draw_slot_ids(jax.random.fold_in(key_of[10], 71), 0)
    norm_attn = jnp.clip(1.0 + 0.18 * jax.random.normal(key_of[3], (D,), jnp.float32), 0.099609375, 1.8984375).astype(jnp.bfloat16)
    w_qkv = draw_w_qkv(jax.random.fold_in(key_of[10], 71), 0)
    w_out = scatter_about(key_of[5], (HEADS * HD, D), HD ** -0.5, 0.5, ((0, 16),))
    norm_moe = jnp.clip(1.0 + 0.18 * jax.random.normal(key_of[6], (D,), jnp.float32), 0.099609375, 1.8984375).astype(jnp.bfloat16)
    router_weight = scatter_about(key_of[7], (D, EXPERTS), (16 * D) ** -0.5, 0.02734375)
    w_gate_up = scatter_about(key_of[8], (EXPERTS, D, 2, FFE), D ** -0.5, 0.109375, ((0, 8), (3, 16)))
    w_down = scatter_about(key_of[9], (EXPERTS, FFE, D), (FFE // 16) ** -0.5, 0.21875, ((0, 8), (1, 16)))
    return dict(tokens=tokens, expert_ids=expert_ids, slot_ids=slot_ids, norm_attn=norm_attn, w_qkv=w_qkv, w_out=w_out, norm_moe=norm_moe, router_weight=router_weight, w_gate_up=w_gate_up, w_down=w_down)


EPS = 1e-05

def rms_norm(values, gain):
    mean_square = lax.optimization_barrier(jnp.mean(values * values, axis=-1, keepdims=True))
    return values * lax.rsqrt(mean_square + EPS) * gain.astype(jnp.float32)

def rotate(values, positions):
    half_dim = values.shape[-1] // 2
    frequencies = jnp.exp(-jnp.log(10000.0) * jnp.arange(half_dim, dtype=jnp.float32) / half_dim)
    angles = positions.astype(jnp.float32)[:, None] * frequencies[None, :]
    cosine_part = jnp.cos(angles)[:, None, :]
    sine_part = jnp.sin(angles)[:, None, :]
    lower_half = values[..., :half_dim]
    upper_half = values[..., half_dim:]
    return jnp.concatenate([lower_half * cosine_part - upper_half * sine_part, lower_half * sine_part + upper_half * cosine_part], axis=-1)

def attend(sequence, norm_attn, w_qkv, w_out):
    normalized_rows = rms_norm(sequence.astype(jnp.float32), norm_attn).astype(jnp.bfloat16)
    qkv = jnp.dot(normalized_rows, w_qkv.reshape(D, 3 * HEADS * HD), preferred_element_type=jnp.float32).reshape(LEN, 3, HEADS, HD)
    positions = jnp.arange(LEN, dtype=jnp.int32)
    queries = rotate(qkv[:, 0], positions).astype(jnp.bfloat16)
    key_rows = rotate(qkv[:, 1], positions).astype(jnp.bfloat16)
    value_rows = qkv[:, 2].astype(jnp.bfloat16)
    scores = jnp.einsum('qhd,khd->hqk', queries.astype(jnp.float32), key_rows.astype(jnp.float32)) * HD ** (-0.5)
    allowed = positions[None, :] <= positions[:, None]
    scores = jnp.where(allowed[None], scores, -1e+30)
    row_max = lax.optimization_barrier(jnp.max(scores, axis=-1, keepdims=True))
    weights = jnp.exp(scores - row_max)
    probabilities = (weights / lax.optimization_barrier(jnp.sum(weights, axis=-1, keepdims=True))).astype(jnp.bfloat16)
    combined = jnp.einsum('hqk,khd->qhd', probabilities.astype(jnp.float32), value_rows.astype(jnp.float32))
    combined = combined.astype(jnp.bfloat16).reshape(LEN, HEADS * HD)
    return jnp.dot(combined, w_out, preferred_element_type=jnp.float32)

def reference(tokens, expert_ids, slot_ids, norm_attn, w_qkv, w_out, norm_moe, router_weight, w_gate_up, w_down):
    attn_out = lax.map(lambda sequence: attend(sequence, norm_attn, w_qkv, w_out), tokens)
    residual = (tokens.astype(jnp.float32) + attn_out).astype(jnp.bfloat16)
    normalized_rows = rms_norm(residual.astype(jnp.float32), norm_moe).astype(jnp.bfloat16)
    router_logit_rows = jnp.einsum('txm,mb->txb', normalized_rows.astype(jnp.float32), router_weight.astype(jnp.float32))
    picked = jnp.take_along_axis(router_logit_rows, expert_ids, axis=-1).reshape(-1, 2)
    weight_one = 1.0 / (1.0 + jnp.exp(picked[:, 1] - picked[:, 0]))
    weight_two = 1.0 / (1.0 + jnp.exp(picked[:, 0] - picked[:, 1]))
    blocks = SEQS * LEN // TOK_DEV
    block_of = jnp.arange(SEQS * LEN, dtype=jnp.int32) // TOK_DEV
    flat_ids = expert_ids.reshape(-1, 2)
    flat_slots = slot_ids.reshape(-1, 2)
    kept = (flat_slots < CAP).astype(jnp.float32)
    safe_slots = jnp.minimum(flat_slots, CAP - 1).astype(jnp.int32)
    row_block = normalized_rows.reshape(-1, D)
    buffers = jnp.zeros((EXPERTS, blocks, CAP, D), jnp.bfloat16)
    buffers = buffers.at[flat_ids[:, 0], block_of, flat_slots[:, 0]].set(row_block, mode='drop')
    buffers = buffers.at[flat_ids[:, 1], block_of, flat_slots[:, 1]].set(row_block, mode='drop')

    def run_expert(operands):
        slots_in, gate_up, down_proj = operands
        hidden = jnp.dot(slots_in.reshape(-1, D), gate_up.reshape(D, 2 * FFE), preferred_element_type=jnp.float32)
        hidden = hidden.reshape(-1, 2, FFE)
        hidden = (jax.nn.silu(hidden[:, 0]) * hidden[:, 1]).astype(jnp.bfloat16)
        return jnp.dot(hidden, down_proj, preferred_element_type=jnp.float32).reshape(blocks, CAP, D)
    results = lax.map(run_expert, (buffers, w_gate_up, w_down))
    result_one = results[flat_ids[:, 0], block_of, safe_slots[:, 0]] * kept[:, 0:1]
    result_two = results[flat_ids[:, 1], block_of, safe_slots[:, 1]] * kept[:, 1:2]
    expert_mix = weight_one[:, None] * result_one + weight_two[:, None] * result_two
    layer_out = residual.astype(jnp.float32).reshape(-1, D) + expert_mix
    return layer_out.astype(jnp.bfloat16).reshape(SEQS, LEN, D)
```

```python
import jax
import jax.numpy as jnp
from jax import lax
from jax.sharding import Mesh
from jax.sharding import PartitionSpec as P

HD = 128
EPS = 1e-05
NEXT_Y = [(i, (i + 1) % 4) for i in range(4)]
PREV_Y = [(i, (i + 3) % 4) for i in range(4)]
PAIR = [(0, 1), (1, 0)]

bf16 = jnp.bfloat16
f32 = jnp.float32


def to_next(v):
    return lax.ppermute(v, "y", NEXT_Y)


def to_prev(v):
    return lax.ppermute(v, "y", PREV_Y)


def to_side(v):
    return lax.ppermute(v, "xl", PAIR)


def to_core(v):
    return lax.ppermute(v, "core", PAIR)


def cat(*parts):
    return jnp.concatenate(parts, axis=0)


def gather_rows(x):
    h = x.shape[0] // 2
    q = h // 2
    a, b = x[:h], x[h:]
    a_side = to_side(a)
    b_m = to_next(b)
    b_p = to_prev(b)
    aa = cat(a, a_side)
    aa_m = to_next(aa)
    aa_p = to_prev(aa)
    b_2a = to_next(b_m[:q])
    b_2b = to_prev(b_p[q:])
    b_side = to_side(b)
    b_mp_side = to_side(cat(b_m, b_p))
    a_2a = to_next(aa_m[:h])
    a_2b = to_prev(aa_p[h:])
    b_2 = cat(b_2a, b_2b)
    b_2_side = to_side(b_2)
    return cat(aa, aa_m, aa_p, a_2a, a_2b, b, b_m, b_p, b_2, b_side, b_mp_side, b_2_side)


def piece_origins():
    out = []
    for dy in (0, 3, 1, 2):
        out += [(dy, 0, 0), (dy, 1, 0)]
    for dx in (0, 1):
        out += [(dy, dx, 1) for dy in (0, 3, 1, 2)]
    return out


def add(a, b):
    return (a.astype(f32) + b.astype(f32)).astype(bf16)


def scatter_rows(x):
    h = x.shape[0] // 16
    q = h // 2
    aa, aa_m, aa_p, a_2a, a_2b = x[: 2 * h], x[2 * h : 4 * h], x[4 * h : 6 * h], x[6 * h : 7 * h], x[7 * h : 8 * h]
    b, b_m, b_p, b_2 = x[8 * h : 9 * h], x[9 * h : 10 * h], x[10 * h : 11 * h], x[11 * h : 12 * h]
    b_side, b_mp_side, b_2_side = x[12 * h : 13 * h], x[13 * h : 15 * h], x[15 * h :]
    r_a = to_prev(a_2a)
    r_b = to_next(a_2b)
    b_2 = add(b_2, to_side(b_2_side))
    r_mp = to_side(b_mp_side)
    r_side = to_side(b_side)
    aa_m = cat(add(aa_m[:h], r_a), aa_m[h:])
    aa_p = cat(aa_p[:h], add(aa_p[h:], r_b))
    r_1 = to_prev(aa_m)
    r_2 = to_next(aa_p)
    s_a = to_prev(b_2[:q])
    s_b = to_next(b_2[q:])
    b_m = add(b_m, r_mp[:h]).astype(f32)
    b_p = add(b_p, r_mp[h:]).astype(f32)
    b_m = cat(b_m[:q] + s_a.astype(f32), b_m[q:]).astype(bf16)
    b_p = cat(b_p[:q], b_p[q:] + s_b.astype(f32)).astype(bf16)
    aa = aa.astype(f32) + r_1.astype(f32) + r_2.astype(f32)
    r_aa = to_side(aa[h:].astype(bf16))
    s_1 = to_prev(b_m)
    s_2 = to_next(b_p)
    out_b = b.astype(f32) + r_side.astype(f32) + s_1.astype(f32) + s_2.astype(f32)
    out_a = aa[:h] + r_aa.astype(f32)
    return cat(out_a, out_b)


def rms_norm(values, gain):
    mean_square = jnp.mean(values * values, axis=-1, keepdims=True)
    return values * lax.rsqrt(mean_square + EPS) * gain.astype(f32)


def rope_tables(positions):
    half = HD // 2
    frequencies = jnp.exp(-jnp.log(10000.0) * jnp.arange(half, dtype=f32) / half)
    angles = positions.astype(f32)[:, None] * frequencies[None, :]
    return jnp.cos(angles)[:, None, :], jnp.sin(angles)[:, None, :]


def rotate(values, cosine, sine):
    half = HD // 2
    lower = values[..., :half]
    upper = values[..., half:]
    return jnp.concatenate([lower * cosine - upper * sine, lower * sine + upper * cosine], axis=-1)


def dot(a, b):
    return jnp.dot(a, b, preferred_element_type=f32)


def exchange_experts(x):
    n, r, w = x.shape
    y = x.reshape(n, r * w // 128, 128)
    y = lax.all_to_all(y, ("z", "xh"), split_axis=0, concat_axis=0, tiled=True)
    return y.reshape(n, r, w)


def body(tokens, expert_ids, slot_ids, norm_attn, w_qkv, w_out, norm_moe, router_weight, w_gate_up, w_down):
    rows = tokens.shape[1]
    width = tokens.shape[2]
    cols = w_qkv.shape[2]
    heads = cols // HD
    y, xl, core = lax.axis_index("y"), lax.axis_index("xl"), lax.axis_index("core")

    residual_in = tokens[0].astype(f32)
    normed = rms_norm(residual_in, norm_attn).astype(bf16)
    seq_rows = gather_rows(normed)
    n_rows = seq_rows.shape[0]

    wq_own = w_qkv.reshape(width, 3 * cols)
    wq_other = to_core(wq_own)
    wo_other = to_core(w_out)
    wgu_own = w_gate_up[0].reshape(width, -1)
    wgu_other = to_core(wgu_own)
    wd_own = w_down[0]
    wd_other = to_core(wd_own)

    starts = jnp.stack(
        [(((y + dy) % 4) * 4 + (xl ^ dx) * 2) * rows + half * (rows // 2) for dy, dx, half in piece_origins()]
    )
    base = (starts[:, None] + jnp.arange(rows // 2, dtype=jnp.int32)[None, :]).reshape(n_rows)
    pos_own = base + core * rows
    pos_other = base + (1 - core) * rows
    cosine, sine = rope_tables(pos_own)

    part_own = dot(seq_rows, wq_own).reshape(n_rows, 3, heads, HD)
    part_other = dot(seq_rows, wq_other).reshape(n_rows, 3, heads, HD)
    q_own = rotate(part_own[:, 0], cosine, sine).astype(bf16)
    q_other = rotate(part_other[:, 0], cosine, sine).astype(bf16)
    k_own = rotate(part_own[:, 1], cosine, sine).astype(bf16)
    k_other = rotate(part_other[:, 1], cosine, sine).astype(bf16)
    v_own = part_own[:, 2].astype(bf16)
    v_other = part_other[:, 2].astype(bf16)
    sent = jnp.stack([k_own, v_own, k_other, v_other])
    got = to_core(sent)
    q_all = jnp.concatenate([q_own, q_other], axis=1)
    k_all = cat(jnp.concatenate([k_own, k_other], axis=1), jnp.concatenate([got[2], got[0]], axis=1))
    v_all = cat(jnp.concatenate([v_own, v_other], axis=1), jnp.concatenate([got[3], got[1]], axis=1))
    pos_keys = cat(pos_own, pos_other)

    scores = jnp.einsum("qhd,khd->hqk", q_all, k_all, preferred_element_type=f32) * HD ** (-0.5)
    allowed = pos_keys[None, :] <= pos_own[:, None]
    scores = jnp.where(allowed[None], scores, -1e30)
    row_max = jnp.max(scores, axis=-1, keepdims=True)
    weights = jnp.exp(scores - row_max)
    probs = (weights / jnp.sum(weights, axis=-1, keepdims=True)).astype(bf16)
    mixed = jnp.einsum("hqk,khd->qhd", probs, v_all, preferred_element_type=f32).astype(bf16)
    mixed_own = mixed[:, :heads].reshape(n_rows, cols)
    mixed_other = mixed[:, heads:].reshape(n_rows, cols)
    attn_part = (dot(mixed_own, w_out) + dot(mixed_other, wo_other)).astype(bf16)
    attn_total = scatter_rows(attn_part)

    residual = (residual_in + attn_total).astype(bf16)
    normed_moe = rms_norm(residual.astype(f32), norm_moe).astype(bf16)
    logits = dot(normed_moe, router_weight)
    experts = router_weight.shape[1]
    capacity = 3 * rows // experts // 2
    chosen = expert_ids[0]
    slot_pos = slot_ids[0]
    labels = jnp.arange(experts, dtype=jnp.int32)
    choose = (chosen[:, :, None] == labels).astype(f32)
    picked = jnp.sum(choose * logits[:, None, :], axis=-1)
    weight_one = 1.0 / (1.0 + jnp.exp(picked[:, 1] - picked[:, 0]))
    weight_two = 1.0 / (1.0 + jnp.exp(picked[:, 0] - picked[:, 1]))
    kept = slot_pos < capacity
    cells = jnp.arange(experts * capacity, dtype=jnp.int32)
    target = jnp.where(kept, chosen * capacity + slot_pos, -1)
    placement = jnp.sum((target[None, :, :] == cells[:, None, None]).astype(jnp.int32), axis=-1).astype(bf16)
    outgoing = dot(placement, normed_moe).astype(bf16).reshape(experts, capacity, width)
    arrived = exchange_experts(outgoing).reshape(experts * capacity, width)

    slots = gather_rows(arrived)

    def gate(w):
        mid = w.shape[1] // 2
        hidden = dot(slots, w)
        return (jax.nn.silu(hidden[:, :mid]) * hidden[:, mid:]).astype(bf16)

    expert_part = (dot(gate(wgu_own), wd_own) + dot(gate(wgu_other), wd_other)).astype(bf16)
    expert_sum = scatter_rows(expert_part).astype(bf16)
    returned = exchange_experts(expert_sum.reshape(experts, capacity, width)).reshape(experts * capacity, width)

    fetched = jnp.take(returned.astype(f32), jnp.maximum(target, 0), axis=0) * kept[:, :, None].astype(f32)
    mix = weight_one[:, None] * fetched[:, 0] + weight_two[:, None] * fetched[:, 1]
    return (residual.astype(f32) + mix).astype(bf16)[None]


def solution(mesh):
    names = ("z", "xh", "y", "xl", "core")
    split = Mesh(mesh.devices.reshape(4, 2, 4, 2, 2), names)
    expert = ("z", "xh")
    tensor = ("y", "xl", "core")
    placed = (
        P(expert, tensor, None),
        P(expert, tensor, None),
        P(expert, tensor, None),
        P(),
        P(None, None, tensor),
        P(tensor, None),
        P(),
        P(),
        P(expert, None, None, tensor),
        P(expert, tensor, None),
    )
    return jax.shard_map(body, mesh=split, in_specs=placed, out_specs=P(expert, tensor, None), check_vma=False)
```

```python
import jax
import jax.numpy as jnp
from jax import lax
from jax.sharding import Mesh
from jax.sharding import PartitionSpec as P

HD = 128
EPS = 1e-05
NEXT_Y = [(i, (i + 1) % 4) for i in range(4)]
PREV_Y = [(i, (i + 3) % 4) for i in range(4)]
PAIR = [(0, 1), (1, 0)]

bf16 = jnp.bfloat16
f32 = jnp.float32


def to_next(v):
    return lax.ppermute(v, "y", NEXT_Y)


def to_prev(v):
    return lax.ppermute(v, "y", PREV_Y)


def to_side(v):
    return lax.ppermute(v, "xl", PAIR)


def to_core(v):
    return lax.ppermute(v, "core", PAIR)


def cat(*parts):
    return jnp.concatenate(parts, axis=0)


def tie(*values):
    return lax.optimization_barrier(values)


def split(x, *parts):
    out, at = [], 0
    for n in parts:
        out.append(x[at : at + n])
        at += n
    return out


def gather_one(x, *beside):
    h = x.shape[0] // 2
    a, b = x[:h], x[h:]
    a_side, b_m, b_p, *beside = tie(to_side(a), to_next(b), to_prev(b), *beside)
    return cat(a, a_side, b, b_m, b_p), beside


def gather_two(one, *beside):
    h = one.shape[0] // 5
    q = h // 2
    aa, bb = one[: 2 * h], one[2 * h :]
    up = cat(aa, one[3 * h : 3 * h + q])
    down = cat(aa, one[4 * h + q :])
    m, p, side, *beside = tie(to_next(up), to_prev(down), to_side(bb), *beside)
    return cat(m, p, side), beside


def gather_three(two, *beside):
    h = two.shape[0] // 8
    q = h // 2
    m, p = two[: 5 * q], two[5 * q : 10 * q]
    far_a, far_b, far_c, *beside = tie(
        to_next(m[:h]), to_prev(p[h : 2 * h]), to_side(cat(m[2 * h :], p[2 * h :])), *beside
    )
    return cat(far_a, far_b, far_c), beside


def origins():
    one = [(0, 0, 0, 2), (0, 1, 0, 2), (0, 0, 2, 2), (3, 0, 2, 2), (1, 0, 2, 2)]
    two = [(3, 0, 0, 2), (3, 1, 0, 2), (2, 0, 2, 1), (1, 0, 0, 2), (1, 1, 0, 2), (2, 0, 3, 1)]
    two += [(0, 1, 2, 2), (3, 1, 2, 2), (1, 1, 2, 2)]
    three = [(2, 0, 0, 2), (2, 1, 0, 2), (2, 1, 2, 2)]
    return one, two, three


def add(a, b):
    return (a.astype(f32) + b.astype(f32)).astype(bf16)


def scatter_three(three):
    h = three.shape[0] // 3
    a, b, c = split(three, h, h, h)
    return tie(to_prev(a), to_next(b), to_side(c))


def scatter_two(two, got):
    h = two.shape[0] // 8
    q = h // 2
    m, p, side = split(two, 5 * q, 5 * q, 6 * q)
    g_a, g_b, g_c = got
    m = cat(add(m[:h], g_a), m[h : 2 * h], add(m[2 * h :], g_c[:q]))
    p = cat(p[:h], add(p[h : 2 * h], g_b), add(p[2 * h :], g_c[q:]))
    return tie(to_prev(m), to_next(p), to_side(side))


def scatter_one(one, got):
    h = one.shape[0] // 5
    q = h // 2
    aa, bb = one[: 2 * h].astype(f32), one[2 * h :].astype(f32)
    g_m, g_p, g_side = [g.astype(f32) for g in got]
    aa = aa + g_m[: 2 * h] + g_p[: 2 * h]
    bb = bb + g_side
    b_m = cat(bb[h : h + q] + g_m[2 * h :], bb[h + q : 2 * h])
    b_p = cat(bb[2 * h : 2 * h + q], bb[2 * h + q :] + g_p[2 * h :])
    l_a, l_m, l_p = tie(to_side(aa[h:].astype(bf16)), to_prev(b_m.astype(bf16)), to_next(b_p.astype(bf16)))
    return cat(aa[:h] + l_a.astype(f32), bb[:h] + l_m.astype(f32) + l_p.astype(f32))


def rms_norm(values, gain):
    mean_square = jnp.mean(values * values, axis=-1, keepdims=True)
    return values * lax.rsqrt(mean_square + EPS) * gain.astype(f32)


def rope_tables(positions):
    half = HD // 2
    frequencies = jnp.exp(-jnp.log(10000.0) * jnp.arange(half, dtype=f32) / half)
    angles = positions.astype(f32)[:, None] * frequencies[None, :]
    return jnp.cos(angles)[:, None, :], jnp.sin(angles)[:, None, :]


def rotate(values, cosine, sine):
    half = HD // 2
    lower = values[..., :half]
    upper = values[..., half:]
    return jnp.concatenate([lower * cosine - upper * sine, lower * sine + upper * cosine], axis=-1)


def dot(a, b):
    return jnp.dot(a, b, preferred_element_type=f32)


def exchange_experts(x):
    n, r, w = x.shape
    y = x.reshape(n, r * w // 128, 128)
    y = lax.all_to_all(y, ("z", "xh"), split_axis=0, concat_axis=0, tiled=True)
    return y.reshape(n, r, w)


def body(tokens, expert_ids, slot_ids, norm_attn, w_qkv, w_out, norm_moe, router_weight, w_gate_up, w_down):
    rows = tokens.shape[1]
    width = tokens.shape[2]
    cols = w_qkv.shape[2]
    heads = cols // HD
    y, xl, core = lax.axis_index("y"), lax.axis_index("xl"), lax.axis_index("core")

    residual_in = tokens[0].astype(f32)
    normed = rms_norm(residual_in, norm_attn).astype(bf16)

    wq_own = w_qkv.reshape(width, 3 * cols)
    wgu_own = w_gate_up[0].reshape(width, -1)
    one, (wq_own,) = gather_one(normed, wq_own)
    wq_other = to_core(wq_own)
    wo_other = to_core(w_out)
    two, (wgu_own,) = gather_two(one, wgu_own)
    three, (wgu_own, wd_own) = gather_three(two, wgu_own, w_down[0])
    wgu_other = to_core(wgu_own)
    wd_other = to_core(wd_own)

    def place(group):
        rows_of = []
        for dy, dx, at, n in group:
            start = (((y + dy) % 4) * 4 + (xl ^ dx) * 2) * rows + at * (rows // 4)
            rows_of.append(start + jnp.arange(n * (rows // 4), dtype=jnp.int32))
        return cat(*rows_of)

    def project(x, base):
        n = x.shape[0]
        cosine, sine = rope_tables(base + core * rows)
        parts = []
        for w in (wq_own, wq_other):
            qkv = dot(x, w).reshape(n, 3, heads, HD)
            parts.append(
                [
                    rotate(qkv[:, 0], cosine, sine).astype(bf16),
                    rotate(qkv[:, 1], cosine, sine).astype(bf16),
                    qkv[:, 2].astype(bf16),
                ]
            )
        (q, k, v), (q2, k2, v2) = parts
        got = to_core(jnp.concatenate([k, k2, v, v2], axis=1))
        k_in = jnp.concatenate([got[:, heads : 2 * heads], got[:, :heads]], axis=1)
        v_in = jnp.concatenate([got[:, 3 * heads :], got[:, 2 * heads : 3 * heads]], axis=1)
        return (
            jnp.concatenate([q, q2], axis=1),
            [jnp.concatenate([k, k2], axis=1), k_in],
            [jnp.concatenate([v, v2], axis=1), v_in],
        )

    bases = [place(g) for g in origins()]
    projected = [project(x, base) for x, base in zip((one, two, three), bases)]
    k_all = cat(*[k for p in projected for k in p[1]])
    v_all = cat(*[v for p in projected for v in p[2]])
    pos_keys = cat(*[pos for base in bases for pos in (base + core * rows, base + (1 - core) * rows)])

    def attend(q, base):
        n = q.shape[0]
        scores = jnp.einsum("qhd,khd->hqk", q, k_all, preferred_element_type=f32) * HD ** (-0.5)
        allowed = pos_keys[None, :] <= (base + core * rows)[:, None]
        scores = jnp.where(allowed[None], scores, -1e30)
        row_max = jnp.max(scores, axis=-1, keepdims=True)
        weights = jnp.exp(scores - row_max)
        probs = (weights / jnp.sum(weights, axis=-1, keepdims=True)).astype(bf16)
        mixed = jnp.einsum("hqk,khd->qhd", probs, v_all, preferred_element_type=f32).astype(bf16)
        mixed_own = mixed[:, :heads].reshape(n, cols)
        mixed_other = mixed[:, heads:].reshape(n, cols)
        return (dot(mixed_own, w_out) + dot(mixed_other, wo_other)).astype(bf16)

    got = scatter_three(attend(projected[2][0], bases[2]))
    got = scatter_two(attend(projected[1][0], bases[1]), got)
    attn_total = scatter_one(attend(projected[0][0], bases[0]), got)

    residual = (residual_in + attn_total).astype(bf16)
    normed_moe = rms_norm(residual.astype(f32), norm_moe).astype(bf16)
    logits = dot(normed_moe, router_weight)
    experts = router_weight.shape[1]
    capacity = 3 * rows // experts // 2
    chosen = expert_ids[0]
    slot_pos = slot_ids[0]
    labels = jnp.arange(experts, dtype=jnp.int32)
    choose = (chosen[:, :, None] == labels).astype(f32)
    picked = jnp.sum(choose * logits[:, None, :], axis=-1)
    weight_one = 1.0 / (1.0 + jnp.exp(picked[:, 1] - picked[:, 0]))
    weight_two = 1.0 / (1.0 + jnp.exp(picked[:, 0] - picked[:, 1]))
    kept = slot_pos < capacity
    cells = jnp.arange(experts * capacity, dtype=jnp.int32)
    target = jnp.where(kept, chosen * capacity + slot_pos, -1)
    placement = jnp.sum((target[None, :, :] == cells[:, None, None]).astype(jnp.int32), axis=-1).astype(bf16)
    outgoing = dot(placement, normed_moe).astype(bf16).reshape(experts, capacity, width)
    arrived = exchange_experts(outgoing).reshape(experts * capacity, width)

    def gate(x, w):
        mid = w.shape[1] // 2
        hidden = dot(x, w)
        return (jax.nn.silu(hidden[:, :mid]) * hidden[:, mid:]).astype(bf16)

    def expert(x):
        return (dot(gate(x, wgu_own), wd_own) + dot(gate(x, wgu_other), wd_other)).astype(bf16)

    one, _ = gather_one(arrived)
    two, _ = gather_two(one)
    part_one = expert(one)
    three, _ = gather_three(two)
    part_two = expert(two)
    got = scatter_three(expert(three))
    got = scatter_two(part_two, got)
    expert_sum = scatter_one(part_one, got).astype(bf16)
    returned = exchange_experts(expert_sum.reshape(experts, capacity, width)).reshape(experts * capacity, width)

    fetched = jnp.take(returned.astype(f32), jnp.maximum(target, 0), axis=0) * kept[:, :, None].astype(f32)
    mix = weight_one[:, None] * fetched[:, 0] + weight_two[:, None] * fetched[:, 1]
    return (residual.astype(f32) + mix).astype(bf16)[None]


def solution(mesh):
    names = ("z", "xh", "y", "xl", "core")
    split = Mesh(mesh.devices.reshape(4, 2, 4, 2, 2), names)
    expert = ("z", "xh")
    tensor = ("y", "xl", "core")
    placed = (
        P(expert, tensor, None),
        P(expert, tensor, None),
        P(expert, tensor, None),
        P(),
        P(None, None, tensor),
        P(tensor, None),
        P(),
        P(),
        P(expert, None, None, tensor),
        P(expert, tensor, None),
    )
    return jax.shard_map(body, mesh=split, in_specs=placed, out_specs=P(expert, tensor, None), check_vma=False)
```

```python
import functools

import jax
import jax.numpy as jnp
from jax import lax
from jax.experimental import pallas as pl
from jax.experimental.pallas import tpu as pltpu
from jax.sharding import Mesh
from jax.sharding import PartitionSpec as P

HD = 128
EPS = 1e-05
NEXT_Y = [(i, (i + 1) % 4) for i in range(4)]
PREV_Y = [(i, (i + 3) % 4) for i in range(4)]
PAIR = [(0, 1), (1, 0)]

bf16 = jnp.bfloat16
f32 = jnp.float32


def to_next(v):
    return lax.ppermute(v, "y", NEXT_Y)


def to_prev(v):
    return lax.ppermute(v, "y", PREV_Y)


def to_side(v):
    return lax.ppermute(v, "xl", PAIR)


def to_core(v):
    return lax.ppermute(v, "core", PAIR)


def cat(*parts):
    return jnp.concatenate(parts, axis=0)


def tie(*values):
    return lax.optimization_barrier(values)


def split(x, *parts):
    out, at = [], 0
    for n in parts:
        out.append(x[at : at + n])
        at += n
    return out


def gather_one(x, *beside):
    h = x.shape[0] // 2
    a, b = x[:h], x[h:]
    a_side, b_m, b_p, *beside = tie(to_side(a), to_next(b), to_prev(b), *beside)
    return cat(a, a_side, b, b_m, b_p), beside


def gather_two(one, *beside):
    h = one.shape[0] // 5
    q = h // 2
    aa, bb = one[: 2 * h], one[2 * h :]
    up = cat(aa, one[3 * h : 3 * h + q])
    down = cat(aa, one[4 * h + q :])
    m, p, side, *beside = tie(to_next(up), to_prev(down), to_side(bb), *beside)
    return cat(m, p, side), beside


def gather_three(two, *beside):
    h = two.shape[0] // 8
    q = h // 2
    m, p = two[: 5 * q], two[5 * q : 10 * q]
    far_a, far_b, far_c, *beside = tie(
        to_next(m[:h]), to_prev(p[h : 2 * h]), to_side(cat(m[2 * h :], p[2 * h :])), *beside
    )
    return cat(far_a, far_b, far_c), beside


def origins():
    one = [(0, 0, 0, 2), (0, 1, 0, 2), (0, 0, 2, 2), (3, 0, 2, 2), (1, 0, 2, 2)]
    two = [(3, 0, 0, 2), (3, 1, 0, 2), (2, 0, 2, 1), (1, 0, 0, 2), (1, 1, 0, 2), (2, 0, 3, 1)]
    two += [(0, 1, 2, 2), (3, 1, 2, 2), (1, 1, 2, 2)]
    three = [(2, 0, 0, 2), (2, 1, 0, 2), (2, 1, 2, 2)]
    return one, two, three


def add(a, b):
    return (a.astype(f32) + b.astype(f32)).astype(bf16)


def scatter_three(three):
    h = three.shape[0] // 3
    a, b, c = split(three, h, h, h)
    return tie(to_prev(a), to_next(b), to_side(c))


def scatter_two(two, got):
    h = two.shape[0] // 8
    q = h // 2
    m, p, side = split(two, 5 * q, 5 * q, 6 * q)
    g_a, g_b, g_c = got
    m = cat(add(m[:h], g_a), m[h : 2 * h], add(m[2 * h :], g_c[:q]))
    p = cat(p[:h], add(p[h : 2 * h], g_b), add(p[2 * h :], g_c[q:]))
    return tie(to_prev(m), to_next(p), to_side(side))


def scatter_one(one, got):
    h = one.shape[0] // 5
    q = h // 2
    aa, bb = one[: 2 * h].astype(f32), one[2 * h :].astype(f32)
    g_m, g_p, g_side = [g.astype(f32) for g in got]
    aa = aa + g_m[: 2 * h] + g_p[: 2 * h]
    bb = bb + g_side
    b_m = cat(bb[h : h + q] + g_m[2 * h :], bb[h + q : 2 * h])
    b_p = cat(bb[2 * h : 2 * h + q], bb[2 * h + q :] + g_p[2 * h :])
    l_a, l_m, l_p = tie(to_side(aa[h:].astype(bf16)), to_prev(b_m.astype(bf16)), to_next(b_p.astype(bf16)))
    return cat(aa[:h] + l_a.astype(f32), bb[:h] + l_m.astype(f32) + l_p.astype(f32))


def rms_norm(values, gain):
    mean_square = jnp.mean(values * values, axis=-1, keepdims=True)
    return values * lax.rsqrt(mean_square + EPS) * gain.astype(f32)


def rope_tables(positions):
    half = HD // 2
    frequencies = jnp.exp(-jnp.log(10000.0) * jnp.arange(half, dtype=f32) / half)
    angles = positions.astype(f32)[:, None] * frequencies[None, :]
    cosine, sine = jnp.cos(angles), jnp.sin(angles)
    return jnp.concatenate([cosine, cosine], axis=1), jnp.concatenate([-sine, sine], axis=1)


def dot(a, b):
    return jnp.dot(a, b, preferred_element_type=f32)


VMEM = 60 * 1024 * 1024


def project_kernel(x1, x2, x3, w_own, w_other, cos, sin, q_out, kv_out):
    step = pl.program_id(0)
    cols = w_own.shape[1]
    turned = step < 2
    at = 0
    for x in (x1, x2, x3):
        n = x.shape[0]
        c = jnp.where(turned, cos[at : at + n, :], 1.0)
        s = jnp.where(turned, sin[at : at + n, :], 0.0)
        xv = x[...]
        done = []
        for w in (w_own, w_other):
            acc = dot(xv, w[...])
            for j in range(cols // HD):
                part = acc[:, j * HD : (j + 1) * HD]
                done.append((part * c + pltpu.roll(part, HD // 2, 1) * s).astype(bf16))
        done = jnp.concatenate(done, axis=1)

        @pl.when(step == 0)
        def _():
            q_out[at : at + n, :] = done

        @pl.when(step > 0)
        def _():
            kv_out[at : at + n, :] = done

        at += n


def project(groups, w_own, w_other, cos, sin):
    n = sum(x.shape[0] for x in groups)
    width = w_own.shape[0]
    cols = w_own.shape[1] // 3
    whole = lambda x: pl.BlockSpec(x.shape, lambda i: (0, 0))
    return pl.pallas_call(
        project_kernel,
        grid=(3,),
        in_specs=[whole(x) for x in groups]
        + [pl.BlockSpec((width, cols), lambda i: (0, i))] * 2
        + [whole(cos), whole(sin)],
        out_specs=[
            pl.BlockSpec((n, 2 * cols), lambda i: (0, 0)),
            pl.BlockSpec((n, 2 * cols), lambda i: (0, jnp.maximum(i - 1, 0))),
        ],
        out_shape=[jax.ShapeDtypeStruct((n, 2 * cols), bf16), jax.ShapeDtypeStruct((n, 4 * cols), bf16)],
        compiler_params=pltpu.CompilerParams(vmem_limit_bytes=VMEM),
        cost_estimate=pl.CostEstimate(flops=12 * n * width * cols, bytes_accessed=2 * width * (n + 6 * cols), transcendentals=0),
        name="project",
    )(*groups, w_own, w_other, cos, sin)


def attend_kernel(at, n, q, kv_own, kv_got, pos_q, pos_own, pos_got, w_own, w_other, out):
    heads = q.shape[1] // HD
    cols = w_own.shape[0]
    rows_at = pos_q[at : at + n, :]
    seen_own = pos_own[...] <= rows_at
    seen_got = pos_got[...] <= rows_at
    scale = HD ** (-0.5)
    contract = (((1,), (1,)), ((), ()))
    mixed = []
    for h in range(heads):
        g = (h + heads // 2) % heads
        mine, its = slice(h * HD, (h + 1) * HD), slice(g * HD, (g + 1) * HD)
        mine_v = slice((heads + h) * HD, (heads + h + 1) * HD)
        its_v = slice((heads + g) * HD, (heads + g + 1) * HD)
        qh = q[at : at + n, mine]
        s_own = lax.dot_general(qh, kv_own[:, mine], contract, preferred_element_type=f32) * scale
        s_got = lax.dot_general(qh, kv_got[:, its], contract, preferred_element_type=f32) * scale
        s_own = jnp.where(seen_own, s_own, -1e30)
        s_got = jnp.where(seen_got, s_got, -1e30)
        top = jnp.maximum(jnp.max(s_own, axis=-1, keepdims=True), jnp.max(s_got, axis=-1, keepdims=True))
        e_own = jnp.exp(s_own - top)
        e_got = jnp.exp(s_got - top)
        inverse = 1.0 / (jnp.sum(e_own, axis=-1, keepdims=True) + jnp.sum(e_got, axis=-1, keepdims=True))
        o = dot((e_own * inverse).astype(bf16), kv_own[:, mine_v]) + dot((e_got * inverse).astype(bf16), kv_got[:, its_v])
        mixed.append(o.astype(bf16))
    half = cols // HD
    m_own = jnp.concatenate(mixed[:half], axis=1)
    m_other = jnp.concatenate(mixed[half:], axis=1)
    out[...] = (dot(m_own, w_own[...]) + dot(m_other, w_other[...])).astype(bf16)


def attend(at, n, q, kv_own, kv_got, pos_q, pos_own, pos_got, w_own, w_other):
    width = w_own.shape[1]
    keys = 2 * kv_own.shape[0]
    heads = q.shape[1] // HD
    return pl.pallas_call(
        functools.partial(attend_kernel, at, n),
        out_shape=jax.ShapeDtypeStruct((n, width), bf16),
        compiler_params=pltpu.CompilerParams(vmem_limit_bytes=VMEM),
        cost_estimate=pl.CostEstimate(
            flops=4 * n * keys * heads * HD * 4 + 2 * n * heads * HD * width,
            bytes_accessed=2 * (q.size + 2 * kv_own.size + 2 * w_own.size + n * width),
            transcendentals=n * keys * heads,
        ),
        name="attend",
    )(q, kv_own, kv_got, pos_q, pos_own, pos_got, w_own, w_other)


def exchange_experts(x):
    n, r, w = x.shape
    y = x.reshape(n, r * w // 128, 128)
    y = lax.all_to_all(y, ("z", "xh"), split_axis=0, concat_axis=0, tiled=True)
    return y.reshape(n, r, w)


def body(tokens, expert_ids, slot_ids, norm_attn, w_qkv, w_out, norm_moe, router_weight, w_gate_up, w_down):
    rows = tokens.shape[1]
    width = tokens.shape[2]
    cols = w_qkv.shape[2]
    y, xl, core = lax.axis_index("y"), lax.axis_index("xl"), lax.axis_index("core")

    residual_in = tokens[0].astype(f32)
    normed = rms_norm(residual_in, norm_attn).astype(bf16)

    def place(group):
        rows_of = []
        for dy, dx, at, n in group:
            start = (((y + dy) % 4) * 4 + (xl ^ dx) * 2) * rows + at * (rows // 4)
            rows_of.append(start + jnp.arange(n * (rows // 4), dtype=jnp.int32))
        return cat(*rows_of)

    wq_own = w_qkv.reshape(width, 3 * cols)
    base = cat(*[place(g) for g in origins()])
    pos_own = base + core * rows
    pos_got = base + (1 - core) * rows
    cos, sin = rope_tables(pos_own)
    one, (wq_own, gate_up, cos, sin) = gather_one(normed, wq_own, w_gate_up, cos, sin)
    wq_other = to_core(wq_own)
    wo_other = to_core(w_out)
    wgu_own = gate_up[0].reshape(width, -1)
    two, (wgu_own,) = gather_two(one, wgu_own)
    three, (wgu_own, wd_own) = gather_three(two, wgu_own, w_down[0])
    wgu_other = to_core(wgu_own)
    wd_other = to_core(wd_own)

    q_all, kv_own = project((one, two, three), wq_own, wq_other, cos, sin)
    kv_got = to_core(kv_own)
    n_one, n_two, n_three = one.shape[0], two.shape[0], three.shape[0]

    def attended(at, n):
        return attend(
            at, n, q_all, kv_own, kv_got, pos_own[:, None], pos_own[None], pos_got[None], w_out, wo_other
        )

    got = scatter_three(attended(n_one + n_two, n_three))
    got = scatter_two(attended(n_one, n_two), got)
    attn_total = scatter_one(attended(0, n_one), got)

    residual = (residual_in + attn_total).astype(bf16)
    normed_moe = rms_norm(residual.astype(f32), norm_moe).astype(bf16)
    logits = dot(normed_moe, router_weight)
    experts = router_weight.shape[1]
    capacity = 3 * rows // experts // 2
    chosen = expert_ids[0]
    slot_pos = slot_ids[0]
    labels = jnp.arange(experts, dtype=jnp.int32)
    choose = (chosen[:, :, None] == labels).astype(f32)
    picked = jnp.sum(choose * logits[:, None, :], axis=-1)
    weight_one = 1.0 / (1.0 + jnp.exp(picked[:, 1] - picked[:, 0]))
    weight_two = 1.0 / (1.0 + jnp.exp(picked[:, 0] - picked[:, 1]))
    kept = slot_pos < capacity
    cells = jnp.arange(experts * capacity, dtype=jnp.int32)
    target = jnp.where(kept, chosen * capacity + slot_pos, -1)
    placement = jnp.sum((target[None, :, :] == cells[:, None, None]).astype(jnp.int32), axis=-1).astype(bf16)
    outgoing = dot(placement, normed_moe).astype(bf16).reshape(experts, capacity, width)
    arrived = exchange_experts(outgoing).reshape(experts * capacity, width)

    def gate(x, w):
        mid = w.shape[1] // 2
        hidden = dot(x, w)
        return (jax.nn.silu(hidden[:, :mid]) * hidden[:, mid:]).astype(bf16)

    def expert(x):
        return (dot(gate(x, wgu_own), wd_own) + dot(gate(x, wgu_other), wd_other)).astype(bf16)

    one, _ = gather_one(arrived)
    two, _ = gather_two(one)
    part_one = expert(one)
    three, _ = gather_three(two)
    part_two = expert(two)
    got = scatter_three(expert(three))
    got = scatter_two(part_two, got)
    expert_sum = scatter_one(part_one, got).astype(bf16)
    returned = exchange_experts(expert_sum.reshape(experts, capacity, width)).reshape(experts * capacity, width)

    fetched = jnp.take(returned.astype(f32), jnp.maximum(target, 0), axis=0) * kept[:, :, None].astype(f32)
    mix = weight_one[:, None] * fetched[:, 0] + weight_two[:, None] * fetched[:, 1]
    return (residual.astype(f32) + mix).astype(bf16)[None]


def solution(mesh):
    names = ("z", "xh", "y", "xl", "core")
    split = Mesh(mesh.devices.reshape(4, 2, 4, 2, 2), names)
    expert = ("z", "xh")
    tensor = ("y", "xl", "core")
    placed = (
        P(expert, tensor, None),
        P(expert, tensor, None),
        P(expert, tensor, None),
        P(),
        P(None, None, tensor),
        P(tensor, None),
        P(),
        P(),
        P(expert, None, None, tensor),
        P(expert, tensor, None),
    )
    return jax.shard_map(body, mesh=split, in_specs=placed, out_specs=P(expert, tensor, None), check_vma=False)
```

```python
import functools

import jax
import jax.numpy as jnp
from jax import lax
from jax.experimental import pallas as pl
from jax.experimental.pallas import tpu as pltpu
from jax.sharding import Mesh
from jax.sharding import PartitionSpec as P

HD = 128
EPS = 1e-05
NEXT_Y = [(i, (i + 1) % 4) for i in range(4)]
PREV_Y = [(i, (i + 3) % 4) for i in range(4)]
PAIR = [(0, 1), (1, 0)]

bf16 = jnp.bfloat16
f32 = jnp.float32


def to_next(v):
    return lax.ppermute(v, "y", NEXT_Y)


def to_prev(v):
    return lax.ppermute(v, "y", PREV_Y)


def to_side(v):
    return lax.ppermute(v, "xl", PAIR)


def to_core(v):
    return lax.ppermute(v, "core", PAIR)


def cat(*parts):
    return jnp.concatenate(parts, axis=0)


def tie(*values):
    return lax.optimization_barrier(values)


def split(x, *parts):
    out, at = [], 0
    for n in parts:
        out.append(x[at : at + n])
        at += n
    return out


def cut(h):
    return h // 2 // 16 * 16


def gather_one(x, *beside):
    h = x.shape[0] // 2
    a, b = x[:h], x[h:]
    a_side, b_m, b_p, *beside = tie(to_side(a), to_next(b), to_prev(b), *beside)
    return (cat(a, a_side), cat(b, b_m, b_p)), beside


def gather_two(one, *beside):
    aa, bb = one
    h = aa.shape[0] // 2
    q = cut(h)
    up = cat(aa, bb[h : h + q])
    down = cat(aa, bb[2 * h + q :])
    m, p, side, *beside = tie(to_next(up), to_prev(down), to_side(bb), *beside)
    return (m, p, side), beside


def gather_three(two, *beside):
    m, p, side = two
    h = side.shape[0] // 3
    far_a, far_b, far_c, *beside = tie(
        to_next(m[:h]), to_prev(p[h : 2 * h]), to_side(cat(m[2 * h :], p[2 * h :])), *beside
    )
    return (far_a, far_b, far_c), beside


def origins():
    one = [(0, 0, 0, 2), (0, 1, 0, 2), (0, 0, 2, 2), (3, 0, 2, 2), (1, 0, 2, 2)]
    two = [(3, 0, 0, 2), (3, 1, 0, 2), (2, 0, 2, 1), (1, 0, 0, 2), (1, 1, 0, 2), (2, 0, 3, 1)]
    two += [(0, 1, 2, 2), (3, 1, 2, 2), (1, 1, 2, 2)]
    three = [(2, 0, 0, 2), (2, 1, 0, 2), (2, 1, 2, 2)]
    return one, two, three


def add(a, b):
    return (a.astype(f32) + b.astype(f32)).astype(bf16)


def scatter_three(three):
    a, b, c = three
    return tie(to_prev(a), to_next(b), to_side(c))


def scatter_two(two, got, *beside):
    m, p, side = two
    h = side.shape[0] // 3
    q = cut(h)
    g_a, g_b, g_c = got
    m = cat(add(m[:h], g_a), m[h : 2 * h], add(m[2 * h :], g_c[:q]))
    p = cat(p[:h], add(p[h : 2 * h], g_b), add(p[2 * h :], g_c[q:]))
    m, p, side, *beside = tie(to_prev(m), to_next(p), to_side(side), *beside)
    return (m, p, side), beside


def scatter_one(one, got):
    aa, bb = [part.astype(f32) for part in one]
    h = aa.shape[0] // 2
    q = cut(h)
    g_m, g_p, g_side = [g.astype(f32) for g in got]
    aa = aa + g_m[: 2 * h] + g_p[: 2 * h]
    bb = bb + g_side
    b_m = cat(bb[h : h + q] + g_m[2 * h :], bb[h + q : 2 * h])
    b_p = cat(bb[2 * h : 2 * h + q], bb[2 * h + q :] + g_p[2 * h :])
    l_a, l_m, l_p = tie(to_side(aa[h:].astype(bf16)), to_prev(b_m.astype(bf16)), to_next(b_p.astype(bf16)))
    return cat(aa[:h] + l_a.astype(f32), bb[:h] + l_m.astype(f32) + l_p.astype(f32))


def rms_norm(values, gain):
    mean_square = jnp.mean(values * values, axis=-1, keepdims=True)
    return values * lax.rsqrt(mean_square + EPS) * gain.astype(f32)


def rope_tables(positions):
    half = HD // 2
    frequencies = jnp.exp(-jnp.log(10000.0) * jnp.arange(half, dtype=f32) / half)
    angles = positions.astype(f32)[:, None] * frequencies[None, :]
    cosine, sine = jnp.cos(angles), jnp.sin(angles)
    return jnp.concatenate([cosine, cosine], axis=1), jnp.concatenate([-sine, sine], axis=1)


def dot(a, b):
    return jnp.dot(a, b, preferred_element_type=f32)


MIB = 1024 * 1024


def project_kernel(turns, *refs):
    *pieces, w_own, w_other, cos, sin, out, rows = refs
    step = pl.program_id(0)
    cols = w_own.shape[2]

    @pl.when(step == 0)
    def _():
        at = 0
        for x in pieces:
            rows[at : at + x.shape[0], :] = x[...]
            at += x.shape[0]

    turned = step < turns
    c = jnp.where(turned, cos[...], 1.0)
    s = jnp.where(turned, sin[...], 0.0)
    done = []
    for w in (w_own, w_other):
        acc = dot(rows[...], w[0])
        for j in range(cols // HD):
            part = acc[:, j * HD : (j + 1) * HD]
            done.append((part * c + pltpu.roll(part, HD // 2, 1) * s).astype(bf16))
    out[...] = jnp.concatenate(done, axis=1)


def project(pieces, w_own, w_other, cos, sin, first, steps, turns):
    n = sum(x.shape[0] for x in pieces)
    width, cols = w_own.shape[1:]
    whole = lambda x: pl.BlockSpec(x.shape, lambda i: (0, 0))
    return pl.pallas_call(
        functools.partial(project_kernel, turns),
        grid=(steps,),
        in_specs=[whole(x) for x in pieces]
        + [pl.BlockSpec((1, width, cols), lambda i: (first + i, 0, 0))] * 2
        + [whole(cos), whole(sin)],
        out_specs=pl.BlockSpec((n, 2 * cols), lambda i: (0, i)),
        out_shape=jax.ShapeDtypeStruct((n, 2 * cols * steps), bf16),
        scratch_shapes=[pltpu.VMEM((n, width), bf16)],
        compiler_params=pltpu.CompilerParams(vmem_limit_bytes=48 * MIB),
        cost_estimate=pl.CostEstimate(
            flops=4 * steps * n * width * cols, bytes_accessed=2 * width * (n + 2 * steps * cols), transcendentals=0
        ),
        name="project",
    )(*pieces, w_own, w_other, cos, sin)


def attend_kernel(at, sizes, q, kv_own, kv_got, pos_q, pos_own, pos_got, w_own, w_other, *outs):
    n = sum(sizes)
    heads = q.shape[1] // HD
    cols = w_own.shape[0]
    rows_at = pos_q[at : at + n, :]
    seen_own = pos_own[...] <= rows_at
    seen_got = pos_got[...] <= rows_at
    scale = HD ** (-0.5)
    contract = (((1,), (1,)), ((), ()))
    mixed = []
    for h in range(heads):
        g = (h + heads // 2) % heads
        mine, its = slice(h * HD, (h + 1) * HD), slice(g * HD, (g + 1) * HD)
        mine_v = slice((heads + h) * HD, (heads + h + 1) * HD)
        its_v = slice((heads + g) * HD, (heads + g + 1) * HD)
        qh = q[at : at + n, mine]
        s_own = lax.dot_general(qh, kv_own[:, mine], contract, preferred_element_type=f32) * scale
        s_got = lax.dot_general(qh, kv_got[:, its], contract, preferred_element_type=f32) * scale
        s_own = jnp.where(seen_own, s_own, -1e30)
        s_got = jnp.where(seen_got, s_got, -1e30)
        top = jnp.maximum(jnp.max(s_own, axis=-1, keepdims=True), jnp.max(s_got, axis=-1, keepdims=True))
        e_own = jnp.exp(s_own - top)
        e_got = jnp.exp(s_got - top)
        inverse = 1.0 / (jnp.sum(e_own, axis=-1, keepdims=True) + jnp.sum(e_got, axis=-1, keepdims=True))
        o = dot((e_own * inverse).astype(bf16), kv_own[:, mine_v]) + dot((e_got * inverse).astype(bf16), kv_got[:, its_v])
        mixed.append(o.astype(bf16))
    half = cols // HD
    m_own = jnp.concatenate(mixed[:half], axis=1)
    m_other = jnp.concatenate(mixed[half:], axis=1)
    total = (dot(m_own, w_own[...]) + dot(m_other, w_other[...])).astype(bf16)
    start = 0
    for out, size in zip(outs, sizes):
        out[...] = total[start : start + size]
        start += size


def attend(at, sizes, q, kv_own, kv_got, pos_q, pos_own, pos_got, w_own, w_other):
    width = w_own.shape[1]
    keys = 2 * kv_own.shape[0]
    n = sum(sizes)
    heads = q.shape[1] // HD
    return pl.pallas_call(
        functools.partial(attend_kernel, at, sizes),
        out_shape=[jax.ShapeDtypeStruct((size, width), bf16) for size in sizes],
        compiler_params=pltpu.CompilerParams(vmem_limit_bytes=28 * MIB),
        cost_estimate=pl.CostEstimate(
            flops=4 * n * keys * heads * HD * 4 + 2 * n * heads * HD * width,
            bytes_accessed=2 * (q.size + 2 * kv_own.size + 2 * w_own.size + n * width),
            transcendentals=n * keys * heads,
        ),
        name="attend",
    )(q, kv_own, kv_got, pos_q, pos_own, pos_got, w_own, w_other)


def expert_kernel(count, *refs):
    pieces, refs = refs[:count], refs[count:]
    (gu_own, gu_other, down_own, down_other), refs = refs[:4], refs[4:]
    outs, (x, gates, downs, hidden, gate_sems, down_sems) = refs[:count], refs[count:]
    tile = gates.shape[3]
    tiles = gu_own.shape[2] // tile
    slots = gates.shape[0]
    mid = down_own.shape[0]
    sides = (gu_own, gu_other)

    def fetch(i):
        side, slot = i // tiles, i % slots
        for number, source in enumerate(sides):

            @pl.when(side == number)
            def _():
                part = source.at[:, :, pl.ds((i % tiles) * tile, tile)]
                pltpu.make_async_copy(part, gates.at[slot], gate_sems.at[slot]).start()

    for i in range(slots - 1):
        fetch(i)
    at = 0
    for piece in pieces:
        x[at : at + piece.shape[0], :] = piece[...]
        at += piece.shape[0]
    to_down = [
        pltpu.make_async_copy(source, downs.at[pl.ds(number * mid, mid), :], down_sems.at[number])
        for number, source in enumerate((down_own, down_other))
    ]

    def step(i, carry):
        slot = i % slots

        @pl.when(i + slots - 1 < 2 * tiles)
        def _():
            fetch(i + slots - 1)

        @pl.when(i == 1)
        def _():
            to_down[0].start()

        @pl.when(i == tiles)
        def _():
            to_down[1].start()

        pltpu.make_async_copy(gu_own.at[:, :, pl.ds(0, tile)], gates.at[slot], gate_sems.at[slot]).wait()
        rows = x[...]
        g = dot(rows, gates[slot, 0])
        u = dot(rows, gates[slot, 1])
        hidden[i] = (g / (1.0 + jnp.exp(-g)) * u).astype(bf16)
        return carry

    lax.fori_loop(0, 2 * tiles, step, 0)
    for copy in to_down:
        copy.wait()
    rows = jnp.concatenate([hidden[i] for i in range(2 * tiles)], axis=1)
    width = x.shape[1]
    for left in range(0, width, width // 4):
        cols = slice(left, left + width // 4)
        part = dot(rows, downs[:, cols]).astype(bf16)
        at = 0
        for out in outs:
            out[:, cols] = part[at : at + out.shape[0]]
            at += out.shape[0]


def expert(pieces, gu_own, gu_other, down_own, down_other):
    n, width = sum(x.shape[0] for x in pieces), pieces[0].shape[1]
    mid = down_own.shape[0]
    tile = 256 if mid % 256 == 0 else mid
    slots = 3
    anywhere = pl.BlockSpec(memory_space=pl.ANY)
    return pl.pallas_call(
        functools.partial(expert_kernel, len(pieces)),
        in_specs=[pl.BlockSpec(memory_space=pltpu.VMEM)] * len(pieces) + [anywhere] * 4,
        out_specs=[pl.BlockSpec(memory_space=pltpu.VMEM)] * len(pieces),
        out_shape=[jax.ShapeDtypeStruct(x.shape, bf16) for x in pieces],
        scratch_shapes=[
            pltpu.VMEM((n, width), bf16),
            pltpu.VMEM((slots, 2, width, tile), bf16),
            pltpu.VMEM((2 * mid, width), bf16),
            pltpu.VMEM((2 * mid // tile, n, tile), bf16),
            pltpu.SemaphoreType.DMA((slots,)),
            pltpu.SemaphoreType.DMA((2,)),
        ],
        compiler_params=pltpu.CompilerParams(vmem_limit_bytes=44 * MIB),
        cost_estimate=pl.CostEstimate(
            flops=12 * n * width * mid, bytes_accessed=2 * (2 * n * width + 6 * width * mid), transcendentals=2 * n * mid
        ),
        name="experts",
    )(*pieces, gu_own, gu_other, down_own, down_other)


def exchange_experts(x):
    n, r, w = x.shape
    y = x.reshape(n, r * w // 128, 128)
    y = lax.all_to_all(y, ("z", "xh"), split_axis=0, concat_axis=0, tiled=True)
    return y.reshape(n, r, w)


def body(tokens, expert_ids, slot_ids, norm_attn, w_qkv, w_out, norm_moe, router_weight, w_gate_up, w_down):
    rows = tokens.shape[1]
    width = tokens.shape[2]
    cols = w_qkv.shape[2]
    y, xl, core = lax.axis_index("y"), lax.axis_index("xl"), lax.axis_index("core")

    residual_in = tokens[0].astype(f32)
    normed = rms_norm(residual_in, norm_attn).astype(bf16)

    def place(group):
        rows_of = []
        for dy, dx, at, n in group:
            start = (((y + dy) % 4) * 4 + (xl ^ dx) * 2) * rows + at * (rows // 4)
            rows_of.append(start + jnp.arange(n * (rows // 4), dtype=jnp.int32))
        return cat(*rows_of)

    wq_own = w_qkv.transpose(1, 0, 2)
    base = cat(*[place(g) for g in origins()])
    pos_own = base + core * rows
    pos_got = base + (1 - core) * rows
    tables = (*rope_tables(pos_own), pos_own[:, None], pos_own[None], pos_got[None])
    one, (wq_own, gate_up, *tables) = gather_one(normed, wq_own, w_gate_up, *tables)
    cos, sin, *places = tables
    wq_other = to_core(wq_own)
    wo_other = to_core(w_out)
    wgu_own = gate_up[0].transpose(1, 0, 2)
    two, (wgu_own, wq_other, wo_other) = gather_two(one, wgu_own, wq_other, wo_other)
    three, _ = gather_three(two)

    pieces = (*one, *two, *three)
    kv_own = project(pieces, wq_own, wq_other, cos, sin, 1, 2, 1)
    kv_got = to_core(kv_own)
    q_all = project(pieces, wq_own, wq_other, cos, sin, 0, 1, 1)
    kv_got, wgu_own, wd_own = tie(kv_got, wgu_own, w_down[0])
    wgu_other = to_core(wgu_own)
    wd_other = to_core(wd_own)
    sizes = [tuple(x.shape[0] for x in group) for group in (one, two, three)]

    def attended(group):
        at = sum(sum(before) for before in sizes[:group])
        return attend(
            at, sizes[group], q_all, kv_own, kv_got, *places, w_out, wo_other
        )

    got = scatter_three(attended(2))
    got, (wgu_other, wd_other) = scatter_two(attended(1), got, wgu_other, wd_other)
    attn_total = scatter_one(attended(0), got)

    residual = (residual_in + attn_total).astype(bf16)
    normed_moe = rms_norm(residual.astype(f32), norm_moe).astype(bf16)
    logits = dot(normed_moe, router_weight)
    experts = router_weight.shape[1]
    capacity = 3 * rows // experts // 2
    chosen = expert_ids[0]
    slot_pos = slot_ids[0]
    labels = jnp.arange(experts, dtype=jnp.int32)
    choose = (chosen[:, :, None] == labels).astype(f32)
    picked = jnp.sum(choose * logits[:, None, :], axis=-1)
    weight_one = 1.0 / (1.0 + jnp.exp(picked[:, 1] - picked[:, 0]))
    weight_two = 1.0 / (1.0 + jnp.exp(picked[:, 0] - picked[:, 1]))
    kept = slot_pos < capacity
    cells = jnp.arange(experts * capacity, dtype=jnp.int32)
    target = jnp.where(kept, chosen * capacity + slot_pos, -1)
    placement = jnp.sum((target[None, :, :] == cells[:, None, None]).astype(jnp.int32), axis=-1).astype(bf16)
    outgoing = dot(placement, normed_moe).astype(bf16).reshape(experts, capacity, width)
    arrived = exchange_experts(outgoing).reshape(experts * capacity, width)

    experts_of = lambda *pieces: expert(pieces, wgu_own, wgu_other, wd_own, wd_other)
    one, _ = gather_one(arrived)
    two, _ = gather_two(one)
    part_one = experts_of(*one)
    three, _ = gather_three(two)
    parts = experts_of(*three, *two)
    got = scatter_three(parts[:3])
    got, _ = scatter_two(parts[3:], got)
    expert_sum = scatter_one(part_one, got).astype(bf16)
    returned = exchange_experts(expert_sum.reshape(experts, capacity, width)).reshape(experts * capacity, width)

    fetched = jnp.take(returned.astype(f32), jnp.maximum(target, 0), axis=0) * kept[:, :, None].astype(f32)
    mix = weight_one[:, None] * fetched[:, 0] + weight_two[:, None] * fetched[:, 1]
    return (residual.astype(f32) + mix).astype(bf16)[None]


def solution(mesh):
    names = ("z", "xh", "y", "xl", "core")
    split = Mesh(mesh.devices.reshape(4, 2, 4, 2, 2), names)
    expert = ("z", "xh")
    tensor = ("y", "xl", "core")
    placed = (
        P(expert, tensor, None),
        P(expert, tensor, None),
        P(expert, tensor, None),
        P(),
        P(None, None, tensor),
        P(tensor, None),
        P(),
        P(),
        P(expert, None, None, tensor),
        P(expert, tensor, None),
    )
    return jax.shard_map(body, mesh=split, in_specs=placed, out_specs=P(expert, tensor, None), check_vma=False)
```

```python
import functools

import jax
import jax.numpy as jnp
from jax import lax
from jax.experimental import pallas as pl
from jax.experimental.pallas import tpu as pltpu
from jax.sharding import Mesh
from jax.sharding import PartitionSpec as P

HD = 128
EPS = 1e-05
NEXT_Y = [(i, (i + 1) % 4) for i in range(4)]
PREV_Y = [(i, (i + 3) % 4) for i in range(4)]
PAIR = [(0, 1), (1, 0)]

bf16 = jnp.bfloat16
f32 = jnp.float32
MIB = 1024 * 1024


def to_next(v):
    return lax.ppermute(v, "y", NEXT_Y)


def to_prev(v):
    return lax.ppermute(v, "y", PREV_Y)


def to_side(v):
    return lax.ppermute(v, "xl", PAIR)


def to_core(v):
    return lax.ppermute(v, "core", PAIR)


def cat(*parts):
    return jnp.concatenate(parts, axis=0)


def tie(*values):
    return lax.optimization_barrier(values)


def split(x, *parts):
    out, at = [], 0
    for n in parts:
        out.append(x[at : at + n])
        at += n
    return out


def cut(h):
    return h // 2 // 16 * 16


def gather_one(x, *beside):
    h = x.shape[0] // 2
    a, b = x[:h], x[h:]
    a_side, b_m, b_p, *beside = tie(to_side(a), to_next(b), to_prev(b), *beside)
    return (cat(a, a_side), cat(b, b_m, b_p)), beside


def gather_two(one, *beside):
    aa, bb = one
    h = aa.shape[0] // 2
    q = cut(h)
    up = cat(aa, bb[h : h + q])
    down = cat(aa, bb[2 * h + q :])
    m, p, side, *beside = tie(to_next(up), to_prev(down), to_side(bb), *beside)
    return (m, p, side), beside


def gather_three(two, *beside):
    m, p, side = two
    h = side.shape[0] // 3
    far_a, far_b, far_c, *beside = tie(
        to_next(m[:h]), to_prev(p[h : 2 * h]), to_side(cat(m[2 * h :], p[2 * h :])), *beside
    )
    return (far_a, far_b, far_c), beside


def origins():
    one = [(0, 0, 0, 2), (0, 1, 0, 2), (0, 0, 2, 2), (3, 0, 2, 2), (1, 0, 2, 2)]
    two = [(3, 0, 0, 2), (3, 1, 0, 2), (2, 0, 2, 1), (1, 0, 0, 2), (1, 1, 0, 2), (2, 0, 3, 1)]
    two += [(0, 1, 2, 2), (3, 1, 2, 2), (1, 1, 2, 2)]
    three = [(2, 0, 0, 2), (2, 1, 0, 2), (2, 1, 2, 2)]
    return one, two, three


def small(kernel, name, outs, *args):
    size = sum(x.size * x.dtype.itemsize for x in (*args, *jax.tree.leaves(outs)))
    return pl.pallas_call(
        kernel,
        out_shape=outs,
        compiler_params=pltpu.CompilerParams(vmem_limit_bytes=28 * MIB),
        cost_estimate=pl.CostEstimate(flops=size, bytes_accessed=size, transcendentals=0),
        name=name,
    )(*args)


def like(rows, x, dtype=bf16):
    return jax.ShapeDtypeStruct((rows, x.shape[1]), dtype)


def scatter_three(three):
    a, b, c = three
    return tie(to_prev(a), to_next(b), to_side(c))


def add_far(h, q, m, p, g_a, g_b, g_c, m_out, p_out):
    plus = lambda a, b: (a.astype(f32) + b.astype(f32)).astype(bf16)
    m_out[:h] = plus(m[:h], g_a[...])
    m_out[h : 2 * h] = m[h : 2 * h]
    m_out[2 * h :] = plus(m[2 * h :], g_c[:q])
    p_out[:h] = p[:h]
    p_out[h : 2 * h] = plus(p[h : 2 * h], g_b[...])
    p_out[2 * h :] = plus(p[2 * h :], g_c[q:])


def scatter_two(two, got):
    m, p, side = two
    h = side.shape[0] // 3
    m, p = small(functools.partial(add_far, h, cut(h)), "add_far", [like(m.shape[0], m), like(p.shape[0], p)], m, p, *got)
    return tie(to_prev(m), to_next(p), to_side(side))


def add_near(h, q, aa, bb, g_m, g_p, g_side, a_out, m_out, p_out, a_keep, b_keep):
    plus = lambda *terms: functools.reduce(jnp.add, [t.astype(f32) for t in terms])
    a_keep[...] = plus(aa[:h], g_m[:h], g_p[:h])
    a_out[...] = plus(aa[h:], g_m[h : 2 * h], g_p[h : 2 * h]).astype(bf16)
    b_keep[...] = plus(bb[:h], g_side[:h])
    m_out[:q] = plus(bb[h : h + q], g_side[h : h + q], g_m[2 * h :]).astype(bf16)
    m_out[q:] = plus(bb[h + q : 2 * h], g_side[h + q : 2 * h]).astype(bf16)
    p_out[:q] = plus(bb[2 * h : 2 * h + q], g_side[2 * h : 2 * h + q]).astype(bf16)
    p_out[q:] = plus(bb[2 * h + q :], g_side[2 * h + q :], g_p[2 * h :]).astype(bf16)


def scatter_one(one, got, *beside):
    aa, bb = one
    h = aa.shape[0] // 2
    outs = [like(h, aa)] * 3 + [like(h, aa, f32)] * 2
    a, m, p, a_keep, b_keep = small(functools.partial(add_near, h, cut(h)), "add_near", outs, aa, bb, *got)
    l_a, l_m, l_p, *beside = tie(to_side(a), to_prev(m), to_next(p), *beside)
    return (a_keep, l_a, b_keep, l_m, l_p), beside


def total_of(a_keep, l_a, b_keep, l_m, l_p):
    top = a_keep[...] + l_a[...].astype(f32)
    low = b_keep[...] + l_m[...].astype(f32) + l_p[...].astype(f32)
    return jnp.concatenate([top, low], axis=0)


def exchange(blocks):
    return lax.all_to_all(blocks, ("z", "xh"), split_axis=0, concat_axis=0, tiled=True)


def columns(g, i):
    return slice((4 * g + i) * HD, (4 * g + i + 1) * HD)


def lines(g, capacity):
    return slice(4 * capacity * g, 4 * capacity * (g + 1))


def one_hot(hit):
    return jnp.where(hit, 1.0, 0.0).astype(bf16)


def line_parts(shape, dim, capacity):
    line = lax.broadcasted_iota(jnp.int32, shape, dim)
    rest = line % (4 * capacity)
    return line // (4 * capacity) * capacity + rest % capacity, rest // capacity


def to_lines(capacity, rows, choose, out):
    for g in range(rows.shape[1] // (4 * HD)):
        stack = jnp.concatenate([rows[:, columns(g, i)] for i in range(4)], axis=0)
        done = dot(choose, stack).astype(bf16)
        for k in range(out.shape[0]):
            out[k, lines(g, capacity), :] = done[4 * capacity * k : 4 * capacity * (k + 1)]


def line_stack(blocks, g, capacity):
    return jnp.concatenate([blocks[k, lines(g, capacity), :] for k in range(blocks.shape[0])], axis=0)


def route_kernel(capacity, tok, a_keep, l_a, b_keep, l_m, l_p, gain, router, ids, cells, res, one, two, out):
    residual = (tok[...].astype(f32) + total_of(a_keep, l_a, b_keep, l_m, l_p)).astype(bf16)
    res[...] = residual
    values = residual.astype(f32)
    scale = lax.rsqrt(jnp.mean(values * values, axis=-1, keepdims=True) + EPS)
    normed = (values * scale * gain[...].astype(f32)).astype(bf16)
    logits = dot(normed, router[...])
    label = lax.broadcasted_iota(jnp.int32, logits.shape, 1)
    first = jnp.sum(jnp.where(label == ids[:, 0:1], logits, 0.0), axis=-1, keepdims=True)
    second = jnp.sum(jnp.where(label == ids[:, 1:2], logits, 0.0), axis=-1, keepdims=True)
    one[...] = 1.0 / (1.0 + jnp.exp(second - first))
    two[...] = 1.0 / (1.0 + jnp.exp(first - second))
    rows = tok.shape[0]
    slot, part = line_parts((4 * capacity * out.shape[0], rows), 0, capacity)
    hit = (slot == cells[0:1, :]) | (slot == cells[1:2, :])
    to_lines(capacity, normed, jnp.concatenate([one_hot(hit & (part == i)) for i in range(4)], axis=1), out)


def unpack_kernel(capacity, blocks, out):
    shape = (out.shape[0], 4 * capacity * blocks.shape[0])
    row = lax.broadcasted_iota(jnp.int32, shape, 0)
    slot, part = line_parts(shape, 1, capacity)
    choose = [one_hot((slot == row) & (part == i)) for i in range(4)]
    for g in range(out.shape[1] // (4 * HD)):
        stack = line_stack(blocks, g, capacity)
        for i in range(4):
            out[:, columns(g, i)] = dot(choose[i], stack).astype(bf16)


def pack_kernel(capacity, a_keep, l_a, b_keep, l_m, l_p, out):
    total = total_of(a_keep, l_a, b_keep, l_m, l_p).astype(bf16)
    shape = (4 * capacity * out.shape[0], total.shape[0])
    row = lax.broadcasted_iota(jnp.int32, shape, 1)
    slot, part = line_parts(shape, 0, capacity)
    choose = jnp.concatenate([one_hot((slot == row) & (part == i)) for i in range(4)], axis=1)
    to_lines(capacity, total, choose, out)


def combine_kernel(capacity, res, one, two, cells, blocks, out):
    slot, part = line_parts((res.shape[0], 4 * capacity * blocks.shape[0]), 1, capacity)
    first = [one_hot((slot == cells[:, 0:1]) & (part == i)) for i in range(4)]
    second = [one_hot((slot == cells[:, 1:2]) & (part == i)) for i in range(4)]
    for g in range(out.shape[1] // (4 * HD)):
        stack = line_stack(blocks, g, capacity)
        for i in range(4):
            mix = one[...] * dot(first[i], stack) + two[...] * dot(second[i], stack)
            out[:, columns(g, i)] = (res[:, columns(g, i)].astype(f32) + mix).astype(bf16)


def rms_norm(values, gain):
    mean_square = jnp.mean(values * values, axis=-1, keepdims=True)
    return values * lax.rsqrt(mean_square + EPS) * gain.astype(f32)


def rope_tables(positions):
    half = HD // 2
    frequencies = jnp.exp(-jnp.log(10000.0) * jnp.arange(half, dtype=f32) / half)
    angles = positions.astype(f32)[:, None] * frequencies[None, :]
    cosine, sine = jnp.cos(angles), jnp.sin(angles)
    return jnp.concatenate([cosine, cosine], axis=1), jnp.concatenate([-sine, sine], axis=1)


def dot(a, b):
    return jnp.dot(a, b, preferred_element_type=f32)


def project_kernel(turns, *refs):
    *pieces, w_own, w_other, cos, sin, out, rows = refs
    step = pl.program_id(0)
    cols = w_own.shape[2]

    @pl.when(step == 0)
    def _():
        at = 0
        for x in pieces:
            rows[at : at + x.shape[0], :] = x[...]
            at += x.shape[0]

    turned = step < turns
    c = jnp.where(turned, cos[...], 1.0)
    s = jnp.where(turned, sin[...], 0.0)
    done = []
    for w in (w_own, w_other):
        acc = dot(rows[...], w[0])
        for j in range(cols // HD):
            part = acc[:, j * HD : (j + 1) * HD]
            done.append((part * c + pltpu.roll(part, HD // 2, 1) * s).astype(bf16))
    out[...] = jnp.concatenate(done, axis=1)


def project(pieces, w_own, w_other, cos, sin, first, steps, turns):
    n = sum(x.shape[0] for x in pieces)
    width, cols = w_own.shape[1:]
    whole = lambda x: pl.BlockSpec(x.shape, lambda i: (0, 0))
    return pl.pallas_call(
        functools.partial(project_kernel, turns),
        grid=(steps,),
        in_specs=[whole(x) for x in pieces]
        + [pl.BlockSpec((1, width, cols), lambda i: (first + i, 0, 0))] * 2
        + [whole(cos), whole(sin)],
        out_specs=pl.BlockSpec((n, 2 * cols), lambda i: (0, i)),
        out_shape=jax.ShapeDtypeStruct((n, 2 * cols * steps), bf16),
        scratch_shapes=[pltpu.VMEM((n, width), bf16)],
        compiler_params=pltpu.CompilerParams(vmem_limit_bytes=48 * MIB),
        cost_estimate=pl.CostEstimate(
            flops=4 * steps * n * width * cols, bytes_accessed=2 * width * (n + 2 * steps * cols), transcendentals=0
        ),
        name="project",
    )(*pieces, w_own, w_other, cos, sin)


def attend_kernel(at, sizes, q, kv_own, kv_got, pos_q, pos_own, pos_got, w_own, w_other, *outs):
    n = sum(sizes)
    heads = q.shape[1] // HD
    cols = w_own.shape[0]
    rows_at = pos_q[at : at + n, :]
    seen_own = pos_own[...] <= rows_at
    seen_got = pos_got[...] <= rows_at
    scale = HD ** (-0.5)
    contract = (((1,), (1,)), ((), ()))
    mixed = []
    for h in range(heads):
        g = (h + heads // 2) % heads
        mine, its = slice(h * HD, (h + 1) * HD), slice(g * HD, (g + 1) * HD)
        mine_v = slice((heads + h) * HD, (heads + h + 1) * HD)
        its_v = slice((heads + g) * HD, (heads + g + 1) * HD)
        qh = q[at : at + n, mine]
        s_own = lax.dot_general(qh, kv_own[:, mine], contract, preferred_element_type=f32) * scale
        s_got = lax.dot_general(qh, kv_got[:, its], contract, preferred_element_type=f32) * scale
        s_own = jnp.where(seen_own, s_own, -1e30)
        s_got = jnp.where(seen_got, s_got, -1e30)
        top = jnp.maximum(jnp.max(s_own, axis=-1, keepdims=True), jnp.max(s_got, axis=-1, keepdims=True))
        e_own = jnp.exp(s_own - top)
        e_got = jnp.exp(s_got - top)
        inverse = 1.0 / (jnp.sum(e_own, axis=-1, keepdims=True) + jnp.sum(e_got, axis=-1, keepdims=True))
        o = dot((e_own * inverse).astype(bf16), kv_own[:, mine_v]) + dot((e_got * inverse).astype(bf16), kv_got[:, its_v])
        mixed.append(o.astype(bf16))
    half = cols // HD
    m_own = jnp.concatenate(mixed[:half], axis=1)
    m_other = jnp.concatenate(mixed[half:], axis=1)
    total = (dot(m_own, w_own[...]) + dot(m_other, w_other[...])).astype(bf16)
    start = 0
    for out, size in zip(outs, sizes):
        out[...] = total[start : start + size]
        start += size


def attend(at, sizes, q, kv_own, kv_got, pos_q, pos_own, pos_got, w_own, w_other):
    width = w_own.shape[1]
    keys = 2 * kv_own.shape[0]
    n = sum(sizes)
    heads = q.shape[1] // HD
    return pl.pallas_call(
        functools.partial(attend_kernel, at, sizes),
        out_shape=[jax.ShapeDtypeStruct((size, width), bf16) for size in sizes],
        compiler_params=pltpu.CompilerParams(vmem_limit_bytes=28 * MIB),
        cost_estimate=pl.CostEstimate(
            flops=4 * n * keys * heads * HD * 4 + 2 * n * heads * HD * width,
            bytes_accessed=2 * (q.size + 2 * kv_own.size + 2 * w_own.size + n * width),
            transcendentals=n * keys * heads,
        ),
        name="attend",
    )(q, kv_own, kv_got, pos_q, pos_own, pos_got, w_own, w_other)


def expert_kernel(count, *refs):
    pieces, refs = refs[:count], refs[count:]
    (gu_own, gu_other, down_own, down_other), refs = refs[:4], refs[4:]
    outs, (x, gates, downs, hidden, gate_sems, down_sems) = refs[:count], refs[count:]
    tile = gates.shape[3]
    tiles = gu_own.shape[2] // tile
    slots = gates.shape[0]
    mid = down_own.shape[0]
    sides = (gu_own, gu_other)

    def fetch(i):
        side, slot = i // tiles, i % slots
        for number, source in enumerate(sides):

            @pl.when(side == number)
            def _():
                part = source.at[:, :, pl.ds((i % tiles) * tile, tile)]
                pltpu.make_async_copy(part, gates.at[slot], gate_sems.at[slot]).start()

    for i in range(slots - 1):
        fetch(i)
    at = 0
    for piece in pieces:
        x[at : at + piece.shape[0], :] = piece[...]
        at += piece.shape[0]
    to_down = [
        pltpu.make_async_copy(source, downs.at[pl.ds(number * mid, mid), :], down_sems.at[number])
        for number, source in enumerate((down_own, down_other))
    ]

    def step(i, carry):
        slot = i % slots

        @pl.when(i + slots - 1 < 2 * tiles)
        def _():
            fetch(i + slots - 1)

        @pl.when(i == 1)
        def _():
            to_down[0].start()

        @pl.when(i == tiles)
        def _():
            to_down[1].start()

        pltpu.make_async_copy(gu_own.at[:, :, pl.ds(0, tile)], gates.at[slot], gate_sems.at[slot]).wait()
        rows = x[...]
        g = dot(rows, gates[slot, 0])
        u = dot(rows, gates[slot, 1])
        hidden[i] = (g / (1.0 + jnp.exp(-g)) * u).astype(bf16)
        return carry

    lax.fori_loop(0, 2 * tiles, step, 0)
    for copy in to_down:
        copy.wait()
    rows = jnp.concatenate([hidden[i] for i in range(2 * tiles)], axis=1)
    width = x.shape[1]
    for left in range(0, width, width // 4):
        cols = slice(left, left + width // 4)
        part = dot(rows, downs[:, cols]).astype(bf16)
        at = 0
        for out in outs:
            out[:, cols] = part[at : at + out.shape[0]]
            at += out.shape[0]


def expert(pieces, gu_own, gu_other, down_own, down_other):
    n, width = sum(x.shape[0] for x in pieces), pieces[0].shape[1]
    mid = down_own.shape[0]
    tile = 256 if mid % 256 == 0 else mid
    slots = 3
    anywhere = pl.BlockSpec(memory_space=pl.ANY)
    return pl.pallas_call(
        functools.partial(expert_kernel, len(pieces)),
        in_specs=[pl.BlockSpec(memory_space=pltpu.VMEM)] * len(pieces) + [anywhere] * 4,
        out_specs=[pl.BlockSpec(memory_space=pltpu.VMEM)] * len(pieces),
        out_shape=[jax.ShapeDtypeStruct(x.shape, bf16) for x in pieces],
        scratch_shapes=[
            pltpu.VMEM((n, width), bf16),
            pltpu.VMEM((slots, 2, width, tile), bf16),
            pltpu.VMEM((2 * mid, width), bf16),
            pltpu.VMEM((2 * mid // tile, n, tile), bf16),
            pltpu.SemaphoreType.DMA((slots,)),
            pltpu.SemaphoreType.DMA((2,)),
        ],
        compiler_params=pltpu.CompilerParams(vmem_limit_bytes=44 * MIB),
        cost_estimate=pl.CostEstimate(
            flops=12 * n * width * mid, bytes_accessed=2 * (2 * n * width + 6 * width * mid), transcendentals=2 * n * mid
        ),
        name="experts",
    )(*pieces, gu_own, gu_other, down_own, down_other)


def body(tokens, expert_ids, slot_ids, norm_attn, w_qkv, w_out, norm_moe, router_weight, w_gate_up, w_down):
    rows = tokens.shape[1]
    width = tokens.shape[2]
    cols = w_qkv.shape[2]
    y, xl, core = lax.axis_index("y"), lax.axis_index("xl"), lax.axis_index("core")

    residual_in = tokens[0].astype(f32)
    normed = rms_norm(residual_in, norm_attn).astype(bf16)

    def place(group):
        rows_of = []
        for dy, dx, at, n in group:
            start = (((y + dy) % 4) * 4 + (xl ^ dx) * 2) * rows + at * (rows // 4)
            rows_of.append(start + jnp.arange(n * (rows // 4), dtype=jnp.int32))
        return cat(*rows_of)

    wq_own = w_qkv.transpose(1, 0, 2)
    base = cat(*[place(g) for g in origins()])
    pos_own = base + core * rows
    pos_got = base + (1 - core) * rows
    experts = router_weight.shape[1]
    capacity = 3 * rows // experts // 2
    cells = jnp.where(slot_ids[0] < capacity, expert_ids[0] * capacity + slot_ids[0], -1)
    tables = (*rope_tables(pos_own), pos_own[:, None], pos_own[None], pos_got[None])
    one, (wq_own, gate_up, *tables) = gather_one(normed, wq_own, w_gate_up, *tables)
    cos, sin, *places = tables
    wq_other = to_core(wq_own)
    wo_other = to_core(w_out)
    wgu_own = gate_up[0].transpose(1, 0, 2)
    two, (wgu_own, wq_other, wo_other) = gather_two(one, wgu_own, wq_other, wo_other)
    three, _ = gather_three(two)

    pieces = (*one, *two, *three)
    kv_own = project(pieces, wq_own, wq_other, cos, sin, 1, 2, 1)
    kv_got = to_core(kv_own)
    q_all = project(pieces, wq_own, wq_other, cos, sin, 0, 1, 1)
    kv_got, q_all, wgu_own, wd_own = tie(kv_got, q_all, wgu_own, w_down[0])
    wgu_other = to_core(wgu_own)
    wd_other = to_core(wd_own)
    sizes = [tuple(x.shape[0] for x in group) for group in (one, two, three)]

    def attended(group):
        at = sum(sum(before) for before in sizes[:group])
        return attend(
            at, sizes[group], q_all, kv_own, kv_got, *places, w_out, wo_other
        )

    got = scatter_three(attended(2))
    got = scatter_two(attended(1), got)
    attn_terms, (wgu_other, wd_other) = scatter_one(attended(0), got, wgu_other, wd_other)

    blocks = jax.ShapeDtypeStruct((experts, capacity * width // HD, HD), bf16)
    residual, weight_one, weight_two, outgoing = small(
        functools.partial(route_kernel, capacity),
        "route",
        [like(rows, tokens[0])] + [jax.ShapeDtypeStruct((rows, 1), f32)] * 2 + [blocks],
        tokens[0],
        *attn_terms,
        norm_moe[None],
        router_weight,
        expert_ids[0],
        cells.T,
    )
    packed = like(experts * capacity, tokens[0])
    arrived = small(functools.partial(unpack_kernel, capacity), "unpack", packed, exchange(outgoing))

    experts_of = lambda *pieces: expert(pieces, wgu_own, wgu_other, wd_own, wd_other)
    one, _ = gather_one(arrived)
    two, _ = gather_two(one)
    part_one = experts_of(*one)
    three, _ = gather_three(two)
    parts = experts_of(*three, *two)
    got = scatter_three(parts[:3])
    got = scatter_two(parts[3:], got)
    expert_terms, _ = scatter_one(part_one, got)
    finished = small(functools.partial(pack_kernel, capacity), "pack", blocks, *expert_terms)
    returned = exchange(finished)
    out = small(
        functools.partial(combine_kernel, capacity),
        "combine",
        like(rows, tokens[0]),
        residual,
        weight_one,
        weight_two,
        cells,
        returned,
    )
    return out[None]


def solution(mesh):
    names = ("z", "xh", "y", "xl", "core")
    split = Mesh(mesh.devices.reshape(4, 2, 4, 2, 2), names)
    expert = ("z", "xh")
    tensor = ("y", "xl", "core")
    placed = (
        P(expert, tensor, None),
        P(expert, tensor, None),
        P(expert, tensor, None),
        P(),
        P(None, None, tensor),
        P(tensor, None),
        P(),
        P(),
        P(expert, None, None, tensor),
        P(expert, tensor, None),
    )
    return jax.shard_map(body, mesh=split, in_specs=placed, out_specs=P(expert, tensor, None), check_vma=False)
```

```python
import functools

import jax
import jax.numpy as jnp
from jax import lax
from jax.experimental import pallas as pl
from jax.experimental.pallas import tpu as pltpu
from jax.sharding import Mesh
from jax.sharding import PartitionSpec as P

HD = 128
EPS = 1e-05
NEXT_Y = [(i, (i + 1) % 4) for i in range(4)]
PREV_Y = [(i, (i + 3) % 4) for i in range(4)]
PAIR = [(0, 1), (1, 0)]

bf16 = jnp.bfloat16
f32 = jnp.float32
MIB = 1024 * 1024


def to_next(v):
    return lax.ppermute(v, "y", NEXT_Y)


def to_prev(v):
    return lax.ppermute(v, "y", PREV_Y)


def to_side(v):
    return lax.ppermute(v, "xl", PAIR)


def to_core(v):
    return lax.ppermute(v, "core", PAIR)


def cat(*parts):
    return jnp.concatenate(parts, axis=0)


def tie(*values):
    return lax.optimization_barrier(values)


def split(x, *parts):
    out, at = [], 0
    for n in parts:
        out.append(x[at : at + n])
        at += n
    return out


def cut(h):
    return h // 2 // 16 * 16


def gather_one(x, *beside):
    h = x.shape[0] // 2
    a, b = x[:h], x[h:]
    a_side, b_m, b_p, *beside = tie(to_side(a), to_next(b), to_prev(b), *beside)
    return (cat(a, a_side), cat(b, b_m, b_p)), beside


def gather_two(one, *beside):
    aa, bb = one
    h = aa.shape[0] // 2
    q = cut(h)
    up = cat(aa, bb[h : h + q])
    down = cat(aa, bb[2 * h + q :])
    m, p, side, *beside = tie(to_next(up), to_prev(down), to_side(bb), *beside)
    return (m, p, side), beside


def gather_three(two, *beside):
    m, p, side = two
    h = side.shape[0] // 3
    far_a, far_b, far_c, *beside = tie(
        to_next(m[:h]), to_prev(p[h : 2 * h]), to_side(cat(m[2 * h :], p[2 * h :])), *beside
    )
    return (far_a, far_b, far_c), beside


def origins():
    one = [(0, 0, 0, 2), (0, 1, 0, 2), (0, 0, 2, 2), (3, 0, 2, 2), (1, 0, 2, 2)]
    two = [(3, 0, 0, 2), (3, 1, 0, 2), (2, 0, 2, 1), (1, 0, 0, 2), (1, 1, 0, 2), (2, 0, 3, 1)]
    two += [(0, 1, 2, 2), (3, 1, 2, 2), (1, 1, 2, 2)]
    three = [(2, 0, 0, 2), (2, 1, 0, 2), (2, 1, 2, 2)]
    return one, two, three


def small(kernel, name, outs, *args):
    size = sum(x.size * x.dtype.itemsize for x in (*args, *jax.tree.leaves(outs)))
    return pl.pallas_call(
        kernel,
        out_shape=outs,
        compiler_params=pltpu.CompilerParams(vmem_limit_bytes=28 * MIB),
        cost_estimate=pl.CostEstimate(flops=size, bytes_accessed=size, transcendentals=0),
        name=name,
    )(*args)


def like(rows, x, dtype=bf16):
    return jax.ShapeDtypeStruct((rows, x.shape[1]), dtype)


def scatter_three(three):
    a, b, c = three
    return tie(to_prev(a), to_next(b), to_side(c))


def add_far(h, q, m, p, g_a, g_b, g_c, m_out, p_out):
    plus = lambda a, b: (a.astype(f32) + b.astype(f32)).astype(bf16)
    m_out[:h] = plus(m[:h], g_a[...])
    m_out[h : 2 * h] = m[h : 2 * h]
    m_out[2 * h :] = plus(m[2 * h :], g_c[:q])
    p_out[:h] = p[:h]
    p_out[h : 2 * h] = plus(p[h : 2 * h], g_b[...])
    p_out[2 * h :] = plus(p[2 * h :], g_c[q:])


def scatter_two(two, got):
    m, p, side = two
    h = side.shape[0] // 3
    m, p = small(functools.partial(add_far, h, cut(h)), "add_far", [like(m.shape[0], m), like(p.shape[0], p)], m, p, *got)
    return tie(to_prev(m), to_next(p), to_side(side))


def add_near(h, q, aa, bb, g_m, g_p, g_side, a_out, m_out, p_out, a_keep, b_keep):
    plus = lambda *terms: functools.reduce(jnp.add, [t.astype(f32) for t in terms])
    a_keep[...] = plus(aa[:h], g_m[:h], g_p[:h])
    a_out[...] = plus(aa[h:], g_m[h : 2 * h], g_p[h : 2 * h]).astype(bf16)
    b_keep[...] = plus(bb[:h], g_side[:h])
    m_out[:q] = plus(bb[h : h + q], g_side[h : h + q], g_m[2 * h :]).astype(bf16)
    m_out[q:] = plus(bb[h + q : 2 * h], g_side[h + q : 2 * h]).astype(bf16)
    p_out[:q] = plus(bb[2 * h : 2 * h + q], g_side[2 * h : 2 * h + q]).astype(bf16)
    p_out[q:] = plus(bb[2 * h + q :], g_side[2 * h + q :], g_p[2 * h :]).astype(bf16)


def scatter_one(one, got, *beside):
    aa, bb = one
    h = aa.shape[0] // 2
    outs = [like(h, aa)] * 3 + [like(h, aa, f32)] * 2
    a, m, p, a_keep, b_keep = small(functools.partial(add_near, h, cut(h)), "add_near", outs, aa, bb, *got)
    l_a, l_m, l_p, *beside = tie(to_side(a), to_prev(m), to_next(p), *beside)
    return (a_keep, l_a, b_keep, l_m, l_p), beside


def total_of(a_keep, l_a, b_keep, l_m, l_p):
    top = a_keep[...] + l_a[...].astype(f32)
    low = b_keep[...] + l_m[...].astype(f32) + l_p[...].astype(f32)
    return jnp.concatenate([top, low], axis=0)


def exchange(blocks):
    return lax.all_to_all(blocks, ("z", "xh"), split_axis=0, concat_axis=0, tiled=True)


def columns(g, i):
    return slice((4 * g + i) * HD, (4 * g + i + 1) * HD)


def lines(g, capacity):
    return slice(4 * capacity * g, 4 * capacity * (g + 1))


def one_hot(hit):
    return jnp.where(hit, 1.0, 0.0).astype(bf16)


def line_parts(shape, dim, capacity):
    line = lax.broadcasted_iota(jnp.int32, shape, dim)
    rest = line % (4 * capacity)
    return line // (4 * capacity) * capacity + rest % capacity, rest // capacity


def to_lines(capacity, rows, choose, out):
    for g in range(rows.shape[1] // (4 * HD)):
        stack = jnp.concatenate([rows[:, columns(g, i)] for i in range(4)], axis=0)
        done = dot(choose, stack).astype(bf16)
        for k in range(out.shape[0]):
            out[k, lines(g, capacity), :] = done[4 * capacity * k : 4 * capacity * (k + 1)]


def line_stack(blocks, g, capacity):
    return jnp.concatenate([blocks[k, lines(g, capacity), :] for k in range(blocks.shape[0])], axis=0)


def route_kernel(capacity, tok, a_keep, l_a, b_keep, l_m, l_p, gain, router, ids, cells, res, one, two, out):
    residual = (tok[...].astype(f32) + total_of(a_keep, l_a, b_keep, l_m, l_p)).astype(bf16)
    res[...] = residual
    values = residual.astype(f32)
    scale = lax.rsqrt(jnp.mean(values * values, axis=-1, keepdims=True) + EPS)
    normed = (values * scale * gain[...].astype(f32)).astype(bf16)
    logits = dot(normed, router[...])
    label = lax.broadcasted_iota(jnp.int32, logits.shape, 1)
    first = jnp.sum(jnp.where(label == ids[:, 0:1], logits, 0.0), axis=-1, keepdims=True)
    second = jnp.sum(jnp.where(label == ids[:, 1:2], logits, 0.0), axis=-1, keepdims=True)
    one[...] = 1.0 / (1.0 + jnp.exp(second - first))
    two[...] = 1.0 / (1.0 + jnp.exp(first - second))
    rows = tok.shape[0]
    slot, part = line_parts((4 * capacity * out.shape[0], rows), 0, capacity)
    hit = (slot == cells[0:1, :]) | (slot == cells[1:2, :])
    to_lines(capacity, normed, jnp.concatenate([one_hot(hit & (part == i)) for i in range(4)], axis=1), out)


def unpack_kernel(capacity, blocks, out):
    shape = (out.shape[0], 4 * capacity * blocks.shape[0])
    row = lax.broadcasted_iota(jnp.int32, shape, 0)
    slot, part = line_parts(shape, 1, capacity)
    choose = [one_hot((slot == row) & (part == i)) for i in range(4)]
    for g in range(out.shape[1] // (4 * HD)):
        stack = line_stack(blocks, g, capacity)
        for i in range(4):
            out[:, columns(g, i)] = dot(choose[i], stack).astype(bf16)


def pack_kernel(capacity, a_keep, l_a, b_keep, l_m, l_p, out):
    total = total_of(a_keep, l_a, b_keep, l_m, l_p).astype(bf16)
    shape = (4 * capacity * out.shape[0], total.shape[0])
    row = lax.broadcasted_iota(jnp.int32, shape, 1)
    slot, part = line_parts(shape, 0, capacity)
    choose = jnp.concatenate([one_hot((slot == row) & (part == i)) for i in range(4)], axis=1)
    to_lines(capacity, total, choose, out)


def combine_kernel(capacity, res, one, two, cells, blocks, out):
    slot, part = line_parts((res.shape[0], 4 * capacity * blocks.shape[0]), 1, capacity)
    first = [one_hot((slot == cells[:, 0:1]) & (part == i)) for i in range(4)]
    second = [one_hot((slot == cells[:, 1:2]) & (part == i)) for i in range(4)]
    for g in range(out.shape[1] // (4 * HD)):
        stack = line_stack(blocks, g, capacity)
        for i in range(4):
            mix = one[...] * dot(first[i], stack) + two[...] * dot(second[i], stack)
            out[:, columns(g, i)] = (res[:, columns(g, i)].astype(f32) + mix).astype(bf16)


def rms_norm(values, gain):
    mean_square = jnp.mean(values * values, axis=-1, keepdims=True)
    return values * lax.rsqrt(mean_square + EPS) * gain.astype(f32)


def rope_tables(positions):
    half = HD // 2
    frequencies = jnp.exp(-jnp.log(10000.0) * jnp.arange(half, dtype=f32) / half)
    angles = positions.astype(f32)[:, None] * frequencies[None, :]
    cosine, sine = jnp.cos(angles), jnp.sin(angles)
    return jnp.concatenate([cosine, cosine], axis=1), jnp.concatenate([-sine, sine], axis=1)


def dot(a, b):
    return jnp.dot(a, b, preferred_element_type=f32)


def project_kernel(turns, *refs):
    *pieces, w_own, w_other, cos, sin, out, rows = refs
    step = pl.program_id(0)
    cols = w_own.shape[2]

    @pl.when(step == 0)
    def _():
        at = 0
        for x in pieces:
            rows[at : at + x.shape[0], :] = x[...]
            at += x.shape[0]

    turned = step < turns
    c = jnp.where(turned, cos[...], 1.0)
    s = jnp.where(turned, sin[...], 0.0)
    done = []
    for w in (w_own, w_other):
        acc = dot(rows[...], w[0])
        for j in range(cols // HD):
            part = acc[:, j * HD : (j + 1) * HD]
            done.append((part * c + pltpu.roll(part, HD // 2, 1) * s).astype(bf16))
    out[...] = jnp.concatenate(done, axis=1)


def project(pieces, w_own, w_other, cos, sin, first, steps, turns):
    n = sum(x.shape[0] for x in pieces)
    width, cols = w_own.shape[1:]
    whole = lambda x: pl.BlockSpec(x.shape, lambda i: (0, 0))
    return pl.pallas_call(
        functools.partial(project_kernel, turns),
        grid=(steps,),
        in_specs=[whole(x) for x in pieces]
        + [pl.BlockSpec((1, width, cols), lambda i: (first + i, 0, 0))] * 2
        + [whole(cos), whole(sin)],
        out_specs=pl.BlockSpec((n, 2 * cols), lambda i: (0, i)),
        out_shape=jax.ShapeDtypeStruct((n, 2 * cols * steps), bf16),
        scratch_shapes=[pltpu.VMEM((n, width), bf16)],
        compiler_params=pltpu.CompilerParams(vmem_limit_bytes=48 * MIB),
        cost_estimate=pl.CostEstimate(
            flops=4 * steps * n * width * cols, bytes_accessed=2 * width * (n + 2 * steps * cols), transcendentals=0
        ),
        name="project",
    )(*pieces, w_own, w_other, cos, sin)


def attend_kernel(at, sizes, q, kv_own, kv_got, pos_q, pos_own, pos_got, w_own, w_other, *refs):
    *outs, near, w, sems = refs
    n = sum(sizes)
    heads = q.shape[1] // HD
    half = heads * HD
    cols = w_own.shape[0]
    routes = [
        (kv_own.at[:, :half], near.at[0]),
        (kv_got.at[:, :half], near.at[1]),
        (kv_own.at[:, half:], near.at[2]),
        (kv_got.at[:, half:], near.at[3]),
        (w_own, w.at[:cols, :]),
        (w_other, w.at[cols:, :]),
    ]
    copies = [pltpu.make_async_copy(a, b, sems.at[i]) for i, (a, b) in enumerate(routes)]
    for copy in copies:
        copy.start()
    rows_at = pos_q[at : at + n, :]
    seen_own = pos_own[...] <= rows_at
    seen_got = pos_got[...] <= rows_at
    scale = HD ** (-0.5)
    contract = (((1,), (1,)), ((), ()))
    copies[0].wait()
    copies[1].wait()
    mixed = []
    for h in range(heads):
        g = (h + heads // 2) % heads
        mine, its = slice(h * HD, (h + 1) * HD), slice(g * HD, (g + 1) * HD)
        qh = q[at : at + n, mine]
        s_own = lax.dot_general(qh, near[0, :, mine], contract, preferred_element_type=f32) * scale
        s_got = lax.dot_general(qh, near[1, :, its], contract, preferred_element_type=f32) * scale
        s_own = jnp.where(seen_own, s_own, -1e30)
        s_got = jnp.where(seen_got, s_got, -1e30)
        top = jnp.maximum(jnp.max(s_own, axis=-1, keepdims=True), jnp.max(s_got, axis=-1, keepdims=True))
        e_own = jnp.exp(s_own - top)
        e_got = jnp.exp(s_got - top)
        inverse = 1.0 / (jnp.sum(e_own, axis=-1, keepdims=True) + jnp.sum(e_got, axis=-1, keepdims=True))
        if h == 0:
            copies[2].wait()
            copies[3].wait()
        o = dot((e_own * inverse).astype(bf16), near[2, :, mine]) + dot((e_got * inverse).astype(bf16), near[3, :, its])
        mixed.append(o.astype(bf16))
    copies[4].wait()
    copies[5].wait()
    total = dot(jnp.concatenate(mixed, axis=1), w[...]).astype(bf16)
    start = 0
    for out, size in zip(outs, sizes):
        out[...] = total[start : start + size]
        start += size


def attend(at, sizes, q, kv_own, kv_got, pos_q, pos_own, pos_got, w_own, w_other):
    cols, width = w_own.shape
    rows = kv_own.shape[0]
    n = sum(sizes)
    heads = q.shape[1] // HD
    near, anywhere = pl.BlockSpec(memory_space=pltpu.VMEM), pl.BlockSpec(memory_space=pl.ANY)
    return pl.pallas_call(
        functools.partial(attend_kernel, at, sizes),
        in_specs=[near, anywhere, anywhere, near, near, near, anywhere, anywhere],
        out_specs=[near] * len(sizes),
        out_shape=[jax.ShapeDtypeStruct((size, width), bf16) for size in sizes],
        scratch_shapes=[
            pltpu.VMEM((4, rows, heads * HD), bf16),
            pltpu.VMEM((2 * cols, width), bf16),
            pltpu.SemaphoreType.DMA((6,)),
        ],
        compiler_params=pltpu.CompilerParams(vmem_limit_bytes=28 * MIB),
        cost_estimate=pl.CostEstimate(
            flops=16 * n * rows * heads * HD + 2 * n * heads * HD * width,
            bytes_accessed=2 * (q.size + 2 * kv_own.size + 2 * w_own.size + n * width),
            transcendentals=2 * n * rows * heads,
        ),
        name="attend",
    )(q, kv_own, kv_got, pos_q, pos_own, pos_got, w_own, w_other)


def expert_kernel(count, sides, added, *refs):
    take = lambda n: (refs[:n], refs[n:])
    pieces, refs = take(count)
    gate_ups, refs = take(sides)
    down_projs, refs = take(sides)
    bases, refs = take(count * added)
    outs, (x, gates, downs, hidden, gate_sems, down_sems) = take(count)
    tile = gates.shape[3]
    tiles = gate_ups[0].shape[2] // tile
    steps = sides * tiles
    slots = gates.shape[0]
    mid = down_projs[0].shape[0]

    def fetch(i):
        side, slot = i // tiles, i % slots
        for number, source in enumerate(gate_ups):

            @pl.when(side == number)
            def _():
                part = source.at[:, :, pl.ds((i % tiles) * tile, tile)]
                pltpu.make_async_copy(part, gates.at[slot], gate_sems.at[slot]).start()

    for i in range(slots - 1):
        fetch(i)
    at = 0
    for piece in pieces:
        x[at : at + piece.shape[0], :] = piece[...]
        at += piece.shape[0]
    to_down = [
        pltpu.make_async_copy(source, downs.at[pl.ds(number * mid, mid), :], down_sems.at[number])
        for number, source in enumerate(down_projs)
    ]

    def step(i, carry):
        slot = i % slots

        @pl.when(i + slots - 1 < steps)
        def _():
            fetch(i + slots - 1)

        for number in range(sides):

            @pl.when(i == (tiles * number if number else min(1, steps - 1)))
            def _():
                to_down[number].start()

        pltpu.make_async_copy(gate_ups[0].at[:, :, pl.ds(0, tile)], gates.at[slot], gate_sems.at[slot]).wait()
        rows = x[...]
        g = dot(rows, gates[slot, 0])
        u = dot(rows, gates[slot, 1])
        hidden[i] = (g / (1.0 + jnp.exp(-g)) * u).astype(bf16)
        return carry

    lax.fori_loop(0, steps, step, 0)
    for copy in to_down:
        copy.wait()
    rows = jnp.concatenate([hidden[i] for i in range(steps)], axis=1)
    width = x.shape[1]
    for left in range(0, width, width // 4):
        cols = slice(left, left + width // 4)
        part = dot(rows, downs[:, cols])
        at = 0
        for j, out in enumerate(outs):
            mine = part[at : at + out.shape[0]]
            if added:
                mine = mine + bases[j][:, cols].astype(f32)
            out[:, cols] = mine.astype(bf16)
            at += out.shape[0]


def expert(pieces, gate_ups, down_projs, bases=()):
    n, width = sum(x.shape[0] for x in pieces), pieces[0].shape[1]
    mid = down_projs[0].shape[0]
    sides = len(gate_ups)
    tile = 256 if mid % 256 == 0 else mid
    slots = 3
    anywhere = pl.BlockSpec(memory_space=pl.ANY)
    near = pl.BlockSpec(memory_space=pltpu.VMEM)
    return pl.pallas_call(
        functools.partial(expert_kernel, len(pieces), sides, int(bool(bases))),
        in_specs=[near] * len(pieces) + [anywhere] * (2 * sides) + [near] * len(bases),
        out_specs=[near] * len(pieces),
        out_shape=[jax.ShapeDtypeStruct(x.shape, bf16) for x in pieces],
        scratch_shapes=[
            pltpu.VMEM((n, width), bf16),
            pltpu.VMEM((slots, 2, width, tile), bf16),
            pltpu.VMEM((sides * mid, width), bf16),
            pltpu.VMEM((sides * mid // tile, n, tile), bf16),
            pltpu.SemaphoreType.DMA((slots,)),
            pltpu.SemaphoreType.DMA((sides,)),
        ],
        compiler_params=pltpu.CompilerParams(vmem_limit_bytes=44 * MIB),
        cost_estimate=pl.CostEstimate(
            flops=6 * sides * n * width * mid,
            bytes_accessed=2 * (2 * n * width + 3 * sides * width * mid),
            transcendentals=sides * n * mid,
        ),
        name="experts",
    )(*pieces, *gate_ups, *down_projs, *bases)


def body(tokens, expert_ids, slot_ids, norm_attn, w_qkv, w_out, norm_moe, router_weight, w_gate_up, w_down):
    rows = tokens.shape[1]
    width = tokens.shape[2]
    cols = w_qkv.shape[2]
    y, xl, core = lax.axis_index("y"), lax.axis_index("xl"), lax.axis_index("core")

    residual_in = tokens[0].astype(f32)
    normed = rms_norm(residual_in, norm_attn).astype(bf16)

    def place(group):
        rows_of = []
        for dy, dx, at, n in group:
            start = (((y + dy) % 4) * 4 + (xl ^ dx) * 2) * rows + at * (rows // 4)
            rows_of.append(start + jnp.arange(n * (rows // 4), dtype=jnp.int32))
        return cat(*rows_of)

    wq_own = w_qkv.transpose(1, 0, 2)
    base = cat(*[place(g) for g in origins()])
    pos_own = base + core * rows
    pos_got = base + (1 - core) * rows
    experts = router_weight.shape[1]
    capacity = 3 * rows // experts // 2
    cells = jnp.where(slot_ids[0] < capacity, expert_ids[0] * capacity + slot_ids[0], -1)
    tables = (*rope_tables(pos_own), pos_own[:, None], pos_own[None], pos_got[None])
    one, (wq_own, gate_up, *tables) = gather_one(normed, wq_own, w_gate_up, *tables)
    cos, sin, *places = tables
    wq_other = to_core(wq_own)
    wo_other = to_core(w_out)
    wgu_own = gate_up[0].transpose(1, 0, 2)
    two, (wgu_own, wq_other, wo_other) = gather_two(one, wgu_own, wq_other, wo_other)
    three, _ = gather_three(two)

    pieces = (*one, *two, *three)
    kv_own = project(pieces, wq_own, wq_other, cos, sin, 1, 2, 1)
    kv_got = to_core(kv_own)
    q_all = project(pieces, wq_own, wq_other, cos, sin, 0, 1, 1)
    kv_got, q_all, wgu_own, wd_own = tie(kv_got, q_all, wgu_own, w_down[0])
    wgu_other = to_core(wgu_own)
    wd_other = to_core(wd_own)
    sizes = [tuple(x.shape[0] for x in group) for group in (one, two, three)]

    def attended(group):
        at = sum(sum(before) for before in sizes[:group])
        return attend(
            at, sizes[group], q_all, kv_own, kv_got, *places, w_out, wo_other
        )

    got = scatter_three(attended(2))
    got = scatter_two(attended(1), got)
    attn_terms, (wgu_other, wd_other) = scatter_one(attended(0), got, wgu_other, wd_other)

    blocks = jax.ShapeDtypeStruct((experts, capacity * width // HD, HD), bf16)
    residual, weight_one, weight_two, outgoing = small(
        functools.partial(route_kernel, capacity),
        "route",
        [like(rows, tokens[0])] + [jax.ShapeDtypeStruct((rows, 1), f32)] * 2 + [blocks],
        tokens[0],
        *attn_terms,
        norm_moe[None],
        router_weight,
        expert_ids[0],
        cells.T,
    )
    packed = like(experts * capacity, tokens[0])
    arrived = small(functools.partial(unpack_kernel, capacity), "unpack", packed, exchange(outgoing))

    both = (wgu_own, wgu_other), (wd_own, wd_other)
    one, _ = gather_one(arrived)
    two, part_one = gather_two(one, *expert(one, *both))
    three, base = gather_three(two, *expert(two, (wgu_own,), (wd_own,)))
    got = scatter_three(expert(three, *both))
    got = scatter_two(expert(two, (wgu_other,), (wd_other,), base), got)
    expert_terms, _ = scatter_one(part_one, got)
    finished = small(functools.partial(pack_kernel, capacity), "pack", blocks, *expert_terms)
    returned = exchange(finished)
    out = small(
        functools.partial(combine_kernel, capacity),
        "combine",
        like(rows, tokens[0]),
        residual,
        weight_one,
        weight_two,
        cells,
        returned,
    )
    return out[None]


def solution(mesh):
    names = ("z", "xh", "y", "xl", "core")
    split = Mesh(mesh.devices.reshape(4, 2, 4, 2, 2), names)
    expert = ("z", "xh")
    tensor = ("y", "xl", "core")
    placed = (
        P(expert, tensor, None),
        P(expert, tensor, None),
        P(expert, tensor, None),
        P(),
        P(None, None, tensor),
        P(tensor, None),
        P(),
        P(),
        P(expert, None, None, tensor),
        P(expert, tensor, None),
    )
    return jax.shard_map(body, mesh=split, in_specs=placed, out_specs=P(expert, tensor, None), check_vma=False)
```

```python
import functools

import jax
import jax.numpy as jnp
from jax import lax
from jax.experimental import pallas as pl
from jax.experimental.pallas import tpu as pltpu
from jax.sharding import Mesh
from jax.sharding import PartitionSpec as P

HD = 128
EPS = 1e-05
NEXT_Y = [(i, (i + 1) % 4) for i in range(4)]
PREV_Y = [(i, (i + 3) % 4) for i in range(4)]
PAIR = [(0, 1), (1, 0)]

bf16 = jnp.bfloat16
f32 = jnp.float32
MIB = 1024 * 1024


def to_next(v):
    return lax.ppermute(v, "y", NEXT_Y)


def to_prev(v):
    return lax.ppermute(v, "y", PREV_Y)


def to_side(v):
    return lax.ppermute(v, "xl", PAIR)


def to_core(v):
    return lax.ppermute(v, "core", PAIR)


def cat(*parts):
    return jnp.concatenate(parts, axis=0)


def tie(*values):
    return lax.optimization_barrier(values)


def split(x, *parts):
    out, at = [], 0
    for n in parts:
        out.append(x[at : at + n])
        at += n
    return out


def cut(h):
    return h // 2 // 16 * 16


def gather_one(x, *beside):
    h = x.shape[0] // 2
    a, b = x[:h], x[h:]
    a_side, b_m, b_p, *beside = tie(to_side(a), to_next(b), to_prev(b), *beside)
    return (cat(a, a_side), b, cat(b_m, b_p), to_side(b)), beside


def gather_two(one, *beside):
    aa, _, b_mp, b_side = one
    h = aa.shape[0] // 2
    q = cut(h)
    up = cat(aa, b_mp[:q])
    down = cat(aa, b_mp[h + q :])
    m, p, b_side, side, *beside = tie(to_next(up), to_prev(down), b_side, to_side(b_mp), *beside)
    return (m, p, b_side, side), beside


def gather_three(two, *beside):
    m, p, side, _ = two
    h = side.shape[0]
    far_a, far_b, far_c, *beside = tie(
        to_next(m[:h]), to_prev(p[h : 2 * h]), to_side(cat(m[2 * h :], p[2 * h :])), *beside
    )
    return (far_a, far_b, far_c), beside


def merged(pieces, at):
    sizes = [x.shape[0] for x in pieces]
    return (*sizes[:at], sum(sizes[at:]))


def origins():
    one = [(0, 0, 0, 2), (0, 1, 0, 2), (0, 0, 2, 2), (3, 0, 2, 2), (1, 0, 2, 2)]
    two = [(3, 0, 0, 2), (3, 1, 0, 2), (2, 0, 2, 1), (1, 0, 0, 2), (1, 1, 0, 2), (2, 0, 3, 1)]
    two += [(0, 1, 2, 2), (3, 1, 2, 2), (1, 1, 2, 2)]
    three = [(2, 0, 0, 2), (2, 1, 0, 2), (2, 1, 2, 2)]
    return one, two, three


def small(kernel, name, outs, *args):
    size = sum(x.size * x.dtype.itemsize for x in (*args, *jax.tree.leaves(outs)))
    return pl.pallas_call(
        kernel,
        out_shape=outs,
        compiler_params=pltpu.CompilerParams(vmem_limit_bytes=28 * MIB),
        cost_estimate=pl.CostEstimate(flops=size, bytes_accessed=size, transcendentals=0),
        name=name,
    )(*args)


def like(rows, x, dtype=bf16):
    return jax.ShapeDtypeStruct((rows, x.shape[1]), dtype)


def scatter_three(three):
    a, b, c = three
    return tie(to_prev(a), to_next(b), to_side(c))


def add_far(h, q, m, p, g_a, g_b, g_c, m_out, p_out):
    plus = lambda a, b: (a.astype(f32) + b.astype(f32)).astype(bf16)
    m_out[:h] = plus(m[:h], g_a[...])
    m_out[h : 2 * h] = m[h : 2 * h]
    m_out[2 * h :] = plus(m[2 * h :], g_c[:q])
    p_out[:h] = p[:h]
    p_out[h : 2 * h] = plus(p[h : 2 * h], g_b[...])
    p_out[2 * h :] = plus(p[2 * h :], g_c[q:])


def scatter_two(two, got):
    m, p, b_side, side = two
    h = b_side.shape[0]
    m, p = small(functools.partial(add_far, h, cut(h)), "add_far", [like(m.shape[0], m), like(p.shape[0], p)], m, p, *got)
    return (*tie(to_prev(m), to_next(p), to_side(side)), to_side(b_side))


def add_near(h, q, aa, bb, g_m, g_p, g_side, a_out, m_out, p_out, a_keep, b_keep):
    plus = lambda *terms: functools.reduce(jnp.add, [t.astype(f32) for t in terms])
    a_keep[...] = plus(aa[:h], g_m[:h], g_p[:h])
    a_out[...] = plus(aa[h:], g_m[h : 2 * h], g_p[h : 2 * h]).astype(bf16)
    b_keep[...] = bb[:h].astype(f32)
    m_out[:q] = plus(bb[h : h + q], g_side[:q], g_m[2 * h :]).astype(bf16)
    m_out[q:] = plus(bb[h + q : 2 * h], g_side[q:h]).astype(bf16)
    p_out[:q] = plus(bb[2 * h : 2 * h + q], g_side[h : h + q]).astype(bf16)
    p_out[q:] = plus(bb[2 * h + q :], g_side[h + q :], g_p[2 * h :]).astype(bf16)


def scatter_one(one, got, *beside):
    aa, bb = one
    h = aa.shape[0] // 2
    outs = [like(h, aa)] * 3 + [like(h, aa, f32)] * 2
    a, m, p, a_keep, b_keep = small(functools.partial(add_near, h, cut(h)), "add_near", outs, aa, bb, *got[:3])
    l_a, l_b, l_m, l_p, *beside = tie(to_side(a), got[3], to_prev(m), to_next(p), *beside)
    return (a_keep, l_a, b_keep, l_b, l_m, l_p), beside


def total_of(a_keep, l_a, b_keep, l_b, l_m, l_p):
    top = a_keep[...] + l_a[...].astype(f32)
    low = b_keep[...] + l_b[...].astype(f32) + l_m[...].astype(f32) + l_p[...].astype(f32)
    return jnp.concatenate([top, low], axis=0)


def exchange(blocks):
    return lax.all_to_all(blocks, ("z", "xh"), split_axis=0, concat_axis=0, tiled=True)


def columns(g, i):
    return slice((4 * g + i) * HD, (4 * g + i + 1) * HD)


def lines(g, capacity):
    return slice(4 * capacity * g, 4 * capacity * (g + 1))


def one_hot(hit):
    return jnp.where(hit, 1.0, 0.0).astype(bf16)


def line_parts(shape, dim, capacity):
    line = lax.broadcasted_iota(jnp.int32, shape, dim)
    rest = line % (4 * capacity)
    return line // (4 * capacity) * capacity + rest % capacity, rest // capacity


def to_lines(capacity, rows, choose, out):
    for g in range(rows.shape[1] // (4 * HD)):
        stack = jnp.concatenate([rows[:, columns(g, i)] for i in range(4)], axis=0)
        done = dot(choose, stack).astype(bf16)
        for k in range(out.shape[0]):
            out[k, lines(g, capacity), :] = done[4 * capacity * k : 4 * capacity * (k + 1)]


def line_stack(blocks, g, capacity):
    return jnp.concatenate([blocks[k, lines(g, capacity), :] for k in range(blocks.shape[0])], axis=0)


def route_kernel(capacity, tok, a_keep, l_a, b_keep, l_b, l_m, l_p, gain, router, ids, cells, res, one, two, out):
    residual = (tok[...].astype(f32) + total_of(a_keep, l_a, b_keep, l_b, l_m, l_p)).astype(bf16)
    res[...] = residual
    values = residual.astype(f32)
    scale = lax.rsqrt(jnp.mean(values * values, axis=-1, keepdims=True) + EPS)
    normed = (values * scale * gain[...].astype(f32)).astype(bf16)
    logits = dot(normed, router[...])
    label = lax.broadcasted_iota(jnp.int32, logits.shape, 1)
    first = jnp.sum(jnp.where(label == ids[:, 0:1], logits, 0.0), axis=-1, keepdims=True)
    second = jnp.sum(jnp.where(label == ids[:, 1:2], logits, 0.0), axis=-1, keepdims=True)
    one[...] = 1.0 / (1.0 + jnp.exp(second - first))
    two[...] = 1.0 / (1.0 + jnp.exp(first - second))
    rows = tok.shape[0]
    slot, part = line_parts((4 * capacity * out.shape[0], rows), 0, capacity)
    hit = (slot == cells[0:1, :]) | (slot == cells[1:2, :])
    to_lines(capacity, normed, jnp.concatenate([one_hot(hit & (part == i)) for i in range(4)], axis=1), out)


def unpack_kernel(capacity, blocks, out):
    shape = (out.shape[0], 4 * capacity * blocks.shape[0])
    row = lax.broadcasted_iota(jnp.int32, shape, 0)
    slot, part = line_parts(shape, 1, capacity)
    choose = [one_hot((slot == row) & (part == i)) for i in range(4)]
    for g in range(out.shape[1] // (4 * HD)):
        stack = line_stack(blocks, g, capacity)
        for i in range(4):
            out[:, columns(g, i)] = dot(choose[i], stack).astype(bf16)


def pack_kernel(capacity, a_keep, l_a, b_keep, l_b, l_m, l_p, out):
    total = total_of(a_keep, l_a, b_keep, l_b, l_m, l_p).astype(bf16)
    shape = (4 * capacity * out.shape[0], total.shape[0])
    row = lax.broadcasted_iota(jnp.int32, shape, 1)
    slot, part = line_parts(shape, 0, capacity)
    choose = jnp.concatenate([one_hot((slot == row) & (part == i)) for i in range(4)], axis=1)
    to_lines(capacity, total, choose, out)


def combine_kernel(capacity, res, one, two, cells, blocks, out):
    slot, part = line_parts((res.shape[0], 4 * capacity * blocks.shape[0]), 1, capacity)
    first = [one_hot((slot == cells[:, 0:1]) & (part == i)) for i in range(4)]
    second = [one_hot((slot == cells[:, 1:2]) & (part == i)) for i in range(4)]
    for g in range(out.shape[1] // (4 * HD)):
        stack = line_stack(blocks, g, capacity)
        for i in range(4):
            mix = one[...] * dot(first[i], stack) + two[...] * dot(second[i], stack)
            out[:, columns(g, i)] = (res[:, columns(g, i)].astype(f32) + mix).astype(bf16)


def rms_norm(values, gain):
    mean_square = jnp.mean(values * values, axis=-1, keepdims=True)
    return values * lax.rsqrt(mean_square + EPS) * gain.astype(f32)


def rope_tables(positions):
    half = HD // 2
    frequencies = jnp.exp(-jnp.log(10000.0) * jnp.arange(half, dtype=f32) / half)
    angles = positions.astype(f32)[:, None] * frequencies[None, :]
    cosine, sine = jnp.cos(angles), jnp.sin(angles)
    return jnp.concatenate([cosine, cosine], axis=1), jnp.concatenate([-sine, sine], axis=1)


def dot(a, b):
    return jnp.dot(a, b, preferred_element_type=f32)


def project_kernel(turns, *refs):
    *pieces, w_own, w_other, cos, sin, out, rows = refs
    step = pl.program_id(0)
    cols = w_own.shape[2]

    @pl.when(step == 0)
    def _():
        at = 0
        for x in pieces:
            rows[at : at + x.shape[0], :] = x[...]
            at += x.shape[0]

    turned = step < turns
    c = jnp.where(turned, cos[...], 1.0)
    s = jnp.where(turned, sin[...], 0.0)
    done = []
    for w in (w_own, w_other):
        acc = dot(rows[...], w[0])
        for j in range(cols // HD):
            part = acc[:, j * HD : (j + 1) * HD]
            done.append((part * c + pltpu.roll(part, HD // 2, 1) * s).astype(bf16))
    out[...] = jnp.concatenate(done, axis=1)


def project(pieces, w_own, w_other, cos, sin, first, steps, turns):
    n = sum(x.shape[0] for x in pieces)
    width, cols = w_own.shape[1:]
    whole = lambda x: pl.BlockSpec(x.shape, lambda i: (0, 0))
    return pl.pallas_call(
        functools.partial(project_kernel, turns),
        grid=(steps,),
        in_specs=[whole(x) for x in pieces]
        + [pl.BlockSpec((1, width, cols), lambda i: (first + i, 0, 0))] * 2
        + [whole(cos), whole(sin)],
        out_specs=pl.BlockSpec((n, 2 * cols), lambda i: (0, i)),
        out_shape=jax.ShapeDtypeStruct((n, 2 * cols * steps), bf16),
        scratch_shapes=[pltpu.VMEM((n, width), bf16)],
        compiler_params=pltpu.CompilerParams(vmem_limit_bytes=48 * MIB),
        cost_estimate=pl.CostEstimate(
            flops=4 * steps * n * width * cols, bytes_accessed=2 * width * (n + 2 * steps * cols), transcendentals=0
        ),
        name="project",
    )(*pieces, w_own, w_other, cos, sin)


def attend_kernel(at, sizes, q, kv_own, kv_got, pos_q, pos_own, pos_got, w_own, w_other, *refs):
    *outs, near, w, sems = refs
    n = sum(sizes)
    heads = q.shape[1] // HD
    half = heads * HD
    cols = w_own.shape[0]
    routes = [
        (kv_own.at[:, :half], near.at[0]),
        (kv_got.at[:, :half], near.at[1]),
        (kv_own.at[:, half:], near.at[2]),
        (kv_got.at[:, half:], near.at[3]),
        (w_own, w.at[:cols, :]),
        (w_other, w.at[cols:, :]),
    ]
    copies = [pltpu.make_async_copy(a, b, sems.at[i]) for i, (a, b) in enumerate(routes)]
    for copy in copies:
        copy.start()
    rows_at = pos_q[at : at + n, :]
    seen_own = pos_own[...] <= rows_at
    seen_got = pos_got[...] <= rows_at
    scale = HD ** (-0.5)
    contract = (((1,), (1,)), ((), ()))
    copies[0].wait()
    copies[1].wait()
    mixed = []
    for h in range(heads):
        g = (h + heads // 2) % heads
        mine, its = slice(h * HD, (h + 1) * HD), slice(g * HD, (g + 1) * HD)
        qh = q[at : at + n, mine]
        s_own = lax.dot_general(qh, near[0, :, mine], contract, preferred_element_type=f32) * scale
        s_got = lax.dot_general(qh, near[1, :, its], contract, preferred_element_type=f32) * scale
        s_own = jnp.where(seen_own, s_own, -1e30)
        s_got = jnp.where(seen_got, s_got, -1e30)
        top = jnp.maximum(jnp.max(s_own, axis=-1, keepdims=True), jnp.max(s_got, axis=-1, keepdims=True))
        e_own = jnp.exp(s_own - top)
        e_got = jnp.exp(s_got - top)
        inverse = 1.0 / (jnp.sum(e_own, axis=-1, keepdims=True) + jnp.sum(e_got, axis=-1, keepdims=True))
        if h == 0:
            copies[2].wait()
            copies[3].wait()
        o = dot((e_own * inverse).astype(bf16), near[2, :, mine]) + dot((e_got * inverse).astype(bf16), near[3, :, its])
        mixed.append(o.astype(bf16))
    copies[4].wait()
    copies[5].wait()
    total = dot(jnp.concatenate(mixed, axis=1), w[...]).astype(bf16)
    start = 0
    for out, size in zip(outs, sizes):
        out[...] = total[start : start + size]
        start += size


def attend(at, sizes, q, kv_own, kv_got, pos_q, pos_own, pos_got, w_own, w_other):
    cols, width = w_own.shape
    rows = kv_own.shape[0]
    n = sum(sizes)
    heads = q.shape[1] // HD
    near, anywhere = pl.BlockSpec(memory_space=pltpu.VMEM), pl.BlockSpec(memory_space=pl.ANY)
    return pl.pallas_call(
        functools.partial(attend_kernel, at, sizes),
        in_specs=[near, anywhere, anywhere, near, near, near, anywhere, anywhere],
        out_specs=[near] * len(sizes),
        out_shape=[jax.ShapeDtypeStruct((size, width), bf16) for size in sizes],
        scratch_shapes=[
            pltpu.VMEM((4, rows, heads * HD), bf16),
            pltpu.VMEM((2 * cols, width), bf16),
            pltpu.SemaphoreType.DMA((6,)),
        ],
        compiler_params=pltpu.CompilerParams(vmem_limit_bytes=28 * MIB),
        cost_estimate=pl.CostEstimate(
            flops=16 * n * rows * heads * HD + 2 * n * heads * HD * width,
            bytes_accessed=2 * (q.size + 2 * kv_own.size + 2 * w_own.size + n * width),
            transcendentals=2 * n * rows * heads,
        ),
        name="attend",
    )(q, kv_own, kv_got, pos_q, pos_own, pos_got, w_own, w_other)


def expert_kernel(count, parts, sides, added, *refs):
    take = lambda n: (refs[:n], refs[n:])
    pieces, refs = take(count)
    gate_ups, refs = take(sides)
    down_projs, refs = take(sides)
    bases, refs = take(parts * added)
    outs, (x, gates, downs, hidden, gate_sems, down_sems) = take(parts)
    tile = gates.shape[3]
    tiles = gate_ups[0].shape[2] // tile
    steps = sides * tiles
    slots = gates.shape[0]
    mid = down_projs[0].shape[0]

    def fetch(i):
        side, slot = i // tiles, i % slots
        for number, source in enumerate(gate_ups):

            @pl.when(side == number)
            def _():
                part = source.at[:, :, pl.ds((i % tiles) * tile, tile)]
                pltpu.make_async_copy(part, gates.at[slot], gate_sems.at[slot]).start()

    for i in range(slots - 1):
        fetch(i)
    at = 0
    for piece in pieces:
        x[at : at + piece.shape[0], :] = piece[...]
        at += piece.shape[0]
    to_down = [
        pltpu.make_async_copy(source, downs.at[pl.ds(number * mid, mid), :], down_sems.at[number])
        for number, source in enumerate(down_projs)
    ]

    def step(i, carry):
        slot = i % slots

        @pl.when(i + slots - 1 < steps)
        def _():
            fetch(i + slots - 1)

        for number in range(sides):

            @pl.when(i == (tiles * number if number else min(1, steps - 1)))
            def _():
                to_down[number].start()

        pltpu.make_async_copy(gate_ups[0].at[:, :, pl.ds(0, tile)], gates.at[slot], gate_sems.at[slot]).wait()
        rows = x[...]
        g = dot(rows, gates[slot, 0])
        u = dot(rows, gates[slot, 1])
        hidden[i] = (g / (1.0 + jnp.exp(-g)) * u).astype(bf16)
        return carry

    lax.fori_loop(0, steps, step, 0)
    for copy in to_down:
        copy.wait()
    rows = jnp.concatenate([hidden[i] for i in range(steps)], axis=1)
    width = x.shape[1]
    for left in range(0, width, width // 4):
        cols = slice(left, left + width // 4)
        part = dot(rows, downs[:, cols])
        at = 0
        for j, out in enumerate(outs):
            mine = part[at : at + out.shape[0]]
            if added:
                mine = mine + bases[j][:, cols].astype(f32)
            out[:, cols] = mine.astype(bf16)
            at += out.shape[0]


def expert(pieces, sizes, gate_ups, down_projs, bases=()):
    n, width = sum(x.shape[0] for x in pieces), pieces[0].shape[1]
    mid = down_projs[0].shape[0]
    sides = len(gate_ups)
    tile = 256 if mid % 256 == 0 else mid
    slots = 3
    anywhere = pl.BlockSpec(memory_space=pl.ANY)
    near = pl.BlockSpec(memory_space=pltpu.VMEM)
    return pl.pallas_call(
        functools.partial(expert_kernel, len(pieces), len(sizes), sides, int(bool(bases))),
        in_specs=[near] * len(pieces) + [anywhere] * (2 * sides) + [near] * len(bases),
        out_specs=[near] * len(sizes),
        out_shape=[jax.ShapeDtypeStruct((size, width), bf16) for size in sizes],
        scratch_shapes=[
            pltpu.VMEM((n, width), bf16),
            pltpu.VMEM((slots, 2, width, tile), bf16),
            pltpu.VMEM((sides * mid, width), bf16),
            pltpu.VMEM((sides * mid // tile, n, tile), bf16),
            pltpu.SemaphoreType.DMA((slots,)),
            pltpu.SemaphoreType.DMA((sides,)),
        ],
        compiler_params=pltpu.CompilerParams(vmem_limit_bytes=44 * MIB),
        cost_estimate=pl.CostEstimate(
            flops=6 * sides * n * width * mid,
            bytes_accessed=2 * (2 * n * width + 3 * sides * width * mid),
            transcendentals=sides * n * mid,
        ),
        name="experts",
    )(*pieces, *gate_ups, *down_projs, *bases)


def body(tokens, expert_ids, slot_ids, norm_attn, w_qkv, w_out, norm_moe, router_weight, w_gate_up, w_down):
    rows = tokens.shape[1]
    width = tokens.shape[2]
    cols = w_qkv.shape[2]
    y, xl, core = lax.axis_index("y"), lax.axis_index("xl"), lax.axis_index("core")

    residual_in = tokens[0].astype(f32)
    normed = rms_norm(residual_in, norm_attn).astype(bf16)

    def place(group):
        rows_of = []
        for dy, dx, at, n in group:
            start = (((y + dy) % 4) * 4 + (xl ^ dx) * 2) * rows + at * (rows // 4)
            rows_of.append(start + jnp.arange(n * (rows // 4), dtype=jnp.int32))
        return cat(*rows_of)

    wq_own = w_qkv.transpose(1, 0, 2)
    base = cat(*[place(g) for g in origins()])
    pos_own = base + core * rows
    pos_got = base + (1 - core) * rows
    experts = router_weight.shape[1]
    capacity = 3 * rows // experts // 2
    cells = jnp.where(slot_ids[0] < capacity, expert_ids[0] * capacity + slot_ids[0], -1)
    tables = (*rope_tables(pos_own), pos_own[:, None], pos_own[None], pos_got[None])
    one, (wq_own, gate_up, *tables) = gather_one(normed, wq_own, w_gate_up, *tables)
    cos, sin, *places = tables
    wq_other = to_core(wq_own)
    wo_other = to_core(w_out)
    wgu_own = gate_up[0].transpose(1, 0, 2)
    two, (wgu_own, wq_other, wo_other) = gather_two(one, wgu_own, wq_other, wo_other)
    three, _ = gather_three(two)

    one = one[:3]
    pieces = (*one, *two, *three)
    kv_own = project(pieces, wq_own, wq_other, cos, sin, 1, 2, 1)
    kv_got = to_core(kv_own)
    q_all = project(pieces, wq_own, wq_other, cos, sin, 0, 1, 1)
    kv_got, q_all, wgu_own, wd_own = tie(kv_got, q_all, wgu_own, w_down[0])
    wgu_other = to_core(wgu_own)
    wd_other = to_core(wd_own)
    sizes = [merged(one, 1), tuple(x.shape[0] for x in two), tuple(x.shape[0] for x in three)]

    def attended(group):
        at = sum(sum(before) for before in sizes[:group])
        return attend(
            at, sizes[group], q_all, kv_own, kv_got, *places, w_out, wo_other
        )

    got = scatter_three(attended(2))
    got = scatter_two(attended(1), got)
    attn_terms, (wgu_other, wd_other) = scatter_one(attended(0), got, wgu_other, wd_other)

    blocks = jax.ShapeDtypeStruct((experts, capacity * width // HD, HD), bf16)
    residual, weight_one, weight_two, outgoing = small(
        functools.partial(route_kernel, capacity),
        "route",
        [like(rows, tokens[0])] + [jax.ShapeDtypeStruct((rows, 1), f32)] * 2 + [blocks],
        tokens[0],
        *attn_terms,
        norm_moe[None],
        router_weight,
        expert_ids[0],
        cells.T,
    )
    packed = like(experts * capacity, tokens[0])
    arrived = small(functools.partial(unpack_kernel, capacity), "unpack", packed, exchange(outgoing))

    both = (wgu_own, wgu_other), (wd_own, wd_other)
    one, _ = gather_one(arrived)
    two, part_one = gather_two(one, *expert(one[:3], merged(one[:3], 1), *both))
    size_two = tuple(x.shape[0] for x in two)
    three, base = gather_three(two, *expert(two, size_two, (wgu_own,), (wd_own,)))
    got = scatter_three(expert(three, tuple(x.shape[0] for x in three), *both))
    got = scatter_two(expert(two, size_two, (wgu_other,), (wd_other,), base), got)
    expert_terms, _ = scatter_one(part_one, got)
    finished = small(functools.partial(pack_kernel, capacity), "pack", blocks, *expert_terms)
    returned = exchange(finished)
    out = small(
        functools.partial(combine_kernel, capacity),
        "combine",
        like(rows, tokens[0]),
        residual,
        weight_one,
        weight_two,
        cells,
        returned,
    )
    return out[None]


def solution(mesh):
    names = ("z", "xh", "y", "xl", "core")
    split = Mesh(mesh.devices.reshape(4, 2, 4, 2, 2), names)
    expert = ("z", "xh")
    tensor = ("y", "xl", "core")
    placed = (
        P(expert, tensor, None),
        P(expert, tensor, None),
        P(expert, tensor, None),
        P(),
        P(None, None, tensor),
        P(tensor, None),
        P(),
        P(),
        P(expert, None, None, tensor),
        P(expert, tensor, None),
    )
    return jax.shard_map(body, mesh=split, in_specs=placed, out_specs=P(expert, tensor, None), check_vma=False)
```

```python
import functools

import jax
import jax.numpy as jnp
from jax import lax
from jax.experimental import pallas as pl
from jax.experimental.pallas import tpu as pltpu
from jax.sharding import Mesh
from jax.sharding import PartitionSpec as P

HD = 128
EPS = 1e-05
NEXT_Y = [(i, (i + 1) % 4) for i in range(4)]
PREV_Y = [(i, (i + 3) % 4) for i in range(4)]
PAIR = [(0, 1), (1, 0)]

bf16 = jnp.bfloat16
f32 = jnp.float32
MIB = 1024 * 1024


def to_next(v):
    return lax.ppermute(v, "y", NEXT_Y)


def to_prev(v):
    return lax.ppermute(v, "y", PREV_Y)


def to_side(v):
    return lax.ppermute(v, "xl", PAIR)


def to_core(v):
    return lax.ppermute(v, "core", PAIR)


def cat(*parts):
    return jnp.concatenate(parts, axis=0)


def tie(*values):
    return lax.optimization_barrier(values)


def split(x, *parts):
    out, at = [], 0
    for n in parts:
        out.append(x[at : at + n])
        at += n
    return out


def cut(h):
    return h // 2 // 16 * 16


def gather_one(x, *beside):
    h = x.shape[0] // 2
    a, b = x[:h], x[h:]
    a_side, b_m, b_p, *beside = tie(to_side(a), to_next(b), to_prev(b), *beside)
    return (cat(a, a_side), b, cat(b_m, b_p), to_side(b)), beside


def gather_two(one, *beside):
    aa, _, b_mp, b_side = one
    h = aa.shape[0] // 2
    q = cut(h)
    up = cat(aa, b_mp[:q])
    down = cat(aa, b_mp[h + q :])
    m, p, b_side, side, *beside = tie(to_next(up), to_prev(down), b_side, to_side(b_mp), *beside)
    return (m, p, b_side, side), beside


def gather_three(two, *beside):
    m, p, side, _ = two
    h = side.shape[0]
    far_a, far_b, far_c, *beside = tie(
        to_next(m[:h]), to_prev(p[h : 2 * h]), to_side(cat(m[2 * h :], p[2 * h :])), *beside
    )
    return (far_a, far_b, far_c), beside


def merged(pieces, at):
    sizes = [x.shape[0] for x in pieces]
    return (*sizes[:at], sum(sizes[at:]))


def origins():
    one = [(0, 0, 0, 2), (0, 1, 0, 2), (0, 0, 2, 2), (3, 0, 2, 2), (1, 0, 2, 2)]
    two = [(3, 0, 0, 2), (3, 1, 0, 2), (2, 0, 2, 1), (1, 0, 0, 2), (1, 1, 0, 2), (2, 0, 3, 1)]
    two += [(0, 1, 2, 2), (3, 1, 2, 2), (1, 1, 2, 2)]
    three = [(2, 0, 0, 2), (2, 1, 0, 2), (2, 1, 2, 2)]
    return one, two, three


def small(kernel, name, outs, *args):
    size = sum(x.size * x.dtype.itemsize for x in (*args, *jax.tree.leaves(outs)))
    return pl.pallas_call(
        kernel,
        out_shape=outs,
        compiler_params=pltpu.CompilerParams(vmem_limit_bytes=28 * MIB),
        cost_estimate=pl.CostEstimate(flops=size, bytes_accessed=size, transcendentals=0),
        name=name,
    )(*args)


def like(rows, x, dtype=bf16):
    return jax.ShapeDtypeStruct((rows, x.shape[1]), dtype)


def scatter_three(three):
    a, b, c = three
    return tie(to_prev(a), to_next(b), to_side(c))


def add_far(h, q, m, p, g_a, g_b, g_c, m_out, p_out):
    plus = lambda a, b: (a.astype(f32) + b.astype(f32)).astype(bf16)
    m_out[:h] = plus(m[:h], g_a[...])
    m_out[h : 2 * h] = m[h : 2 * h]
    m_out[2 * h :] = plus(m[2 * h :], g_c[:q])
    p_out[:h] = p[:h]
    p_out[h : 2 * h] = plus(p[h : 2 * h], g_b[...])
    p_out[2 * h :] = plus(p[2 * h :], g_c[q:])


def scatter_two(two, got):
    m, p, b_side, side = two
    h = b_side.shape[0]
    m, p = small(functools.partial(add_far, h, cut(h)), "add_far", [like(m.shape[0], m), like(p.shape[0], p)], m, p, *got)
    return (*tie(to_prev(m), to_next(p), to_side(side)), to_side(b_side))


def add_near(h, q, aa, bb, g_m, g_p, g_side, a_out, m_out, p_out, a_keep, b_keep):
    plus = lambda *terms: functools.reduce(jnp.add, [t.astype(f32) for t in terms])
    a_keep[...] = plus(aa[:h], g_m[:h], g_p[:h])
    a_out[...] = plus(aa[h:], g_m[h : 2 * h], g_p[h : 2 * h]).astype(bf16)
    b_keep[...] = bb[:h].astype(f32)
    m_out[:q] = plus(bb[h : h + q], g_side[:q], g_m[2 * h :]).astype(bf16)
    m_out[q:] = plus(bb[h + q : 2 * h], g_side[q:h]).astype(bf16)
    p_out[:q] = plus(bb[2 * h : 2 * h + q], g_side[h : h + q]).astype(bf16)
    p_out[q:] = plus(bb[2 * h + q :], g_side[h + q :], g_p[2 * h :]).astype(bf16)


def scatter_one(one, got, *beside):
    aa, bb = one
    h = aa.shape[0] // 2
    outs = [like(h, aa)] * 3 + [like(h, aa, f32)] * 2
    a, m, p, a_keep, b_keep = small(functools.partial(add_near, h, cut(h)), "add_near", outs, aa, bb, *got[:3])
    l_a, l_b, l_m, l_p, *beside = tie(to_side(a), got[3], to_prev(m), to_next(p), *beside)
    return (a_keep, l_a, b_keep, l_b, l_m, l_p), beside


def total_of(a_keep, l_a, b_keep, l_b, l_m, l_p):
    top = a_keep[...] + l_a[...].astype(f32)
    low = b_keep[...] + l_b[...].astype(f32) + l_m[...].astype(f32) + l_p[...].astype(f32)
    return jnp.concatenate([top, low], axis=0)


def exchange(blocks):
    return lax.all_to_all(blocks, ("z", "xh"), split_axis=0, concat_axis=0, tiled=True)


def columns(g, i):
    return slice((4 * g + i) * HD, (4 * g + i + 1) * HD)


def lines(g, capacity):
    return slice(4 * capacity * g, 4 * capacity * (g + 1))


def one_hot(hit):
    return jnp.where(hit, 1.0, 0.0).astype(bf16)


def line_parts(shape, dim, capacity):
    line = lax.broadcasted_iota(jnp.int32, shape, dim)
    rest = line % (4 * capacity)
    return line // (4 * capacity) * capacity + rest % capacity, rest // capacity


def to_lines(capacity, rows, choose, out):
    for g in range(rows.shape[1] // (4 * HD)):
        stack = jnp.concatenate([rows[:, columns(g, i)] for i in range(4)], axis=0)
        done = dot(choose, stack).astype(bf16)
        for k in range(out.shape[0]):
            out[k, lines(g, capacity), :] = done[4 * capacity * k : 4 * capacity * (k + 1)]


def line_stack(blocks, g, capacity):
    return jnp.concatenate([blocks[k, lines(g, capacity), :] for k in range(blocks.shape[0])], axis=0)


def route_kernel(capacity, tok, a_keep, l_a, b_keep, l_b, l_m, l_p, gain, router, ids, cells, res, one, two, out):
    residual = (tok[...].astype(f32) + total_of(a_keep, l_a, b_keep, l_b, l_m, l_p)).astype(bf16)
    res[...] = residual
    values = residual.astype(f32)
    scale = lax.rsqrt(jnp.mean(values * values, axis=-1, keepdims=True) + EPS)
    normed = (values * scale * gain[...].astype(f32)).astype(bf16)
    logits = dot(normed, router[...])
    label = lax.broadcasted_iota(jnp.int32, logits.shape, 1)
    first = jnp.sum(jnp.where(label == ids[:, 0:1], logits, 0.0), axis=-1, keepdims=True)
    second = jnp.sum(jnp.where(label == ids[:, 1:2], logits, 0.0), axis=-1, keepdims=True)
    one[...] = 1.0 / (1.0 + jnp.exp(second - first))
    two[...] = 1.0 / (1.0 + jnp.exp(first - second))
    rows = tok.shape[0]
    slot, part = line_parts((4 * capacity * out.shape[0], rows), 0, capacity)
    hit = (slot == cells[0:1, :]) | (slot == cells[1:2, :])
    to_lines(capacity, normed, jnp.concatenate([one_hot(hit & (part == i)) for i in range(4)], axis=1), out)


def unpack_kernel(capacity, blocks, out):
    shape = (out.shape[0], 4 * capacity * blocks.shape[0])
    row = lax.broadcasted_iota(jnp.int32, shape, 0)
    slot, part = line_parts(shape, 1, capacity)
    choose = [one_hot((slot == row) & (part == i)) for i in range(4)]
    for g in range(out.shape[1] // (4 * HD)):
        stack = line_stack(blocks, g, capacity)
        for i in range(4):
            out[:, columns(g, i)] = dot(choose[i], stack).astype(bf16)


def pack_kernel(capacity, a_keep, l_a, b_keep, l_b, l_m, l_p, out):
    total = total_of(a_keep, l_a, b_keep, l_b, l_m, l_p).astype(bf16)
    shape = (4 * capacity * out.shape[0], total.shape[0])
    row = lax.broadcasted_iota(jnp.int32, shape, 1)
    slot, part = line_parts(shape, 0, capacity)
    choose = jnp.concatenate([one_hot((slot == row) & (part == i)) for i in range(4)], axis=1)
    to_lines(capacity, total, choose, out)


def combine_kernel(capacity, res, one, two, cells, blocks, out):
    slot, part = line_parts((res.shape[0], 4 * capacity * blocks.shape[0]), 1, capacity)
    first = [one_hot((slot == cells[:, 0:1]) & (part == i)) for i in range(4)]
    second = [one_hot((slot == cells[:, 1:2]) & (part == i)) for i in range(4)]
    for g in range(out.shape[1] // (4 * HD)):
        stack = line_stack(blocks, g, capacity)
        for i in range(4):
            mix = one[...] * dot(first[i], stack) + two[...] * dot(second[i], stack)
            out[:, columns(g, i)] = (res[:, columns(g, i)].astype(f32) + mix).astype(bf16)


def norm_kernel(tok, gain, out):
    values = tok[...].astype(f32)
    scale = lax.rsqrt(jnp.mean(values * values, axis=-1, keepdims=True) + EPS)
    out[...] = (values * scale * gain[...].astype(f32)).astype(bf16)


def rope_tables(positions):
    half = HD // 2
    frequencies = jnp.exp(-jnp.log(10000.0) * jnp.arange(half, dtype=f32) / half)
    angles = positions.astype(f32)[:, None] * frequencies[None, :]
    cosine, sine = jnp.cos(angles), jnp.sin(angles)
    return jnp.concatenate([cosine, cosine], axis=1), jnp.concatenate([-sine, sine], axis=1)


def dot(a, b):
    return jnp.dot(a, b, preferred_element_type=f32)


def project_kernel(turns, *refs):
    *pieces, w_own, w_other, cos, sin, out, rows = refs
    step = pl.program_id(0)
    cols = w_own.shape[2]

    @pl.when(step == 0)
    def _():
        at = 0
        for x in pieces:
            rows[at : at + x.shape[0], :] = x[...]
            at += x.shape[0]

    turned = step < turns
    c = jnp.where(turned, cos[...], 1.0)
    s = jnp.where(turned, sin[...], 0.0)
    done = []
    for w in (w_own, w_other):
        acc = dot(rows[...], w[0])
        for j in range(cols // HD):
            part = acc[:, j * HD : (j + 1) * HD]
            done.append((part * c + pltpu.roll(part, HD // 2, 1) * s).astype(bf16))
    out[...] = jnp.concatenate(done, axis=1)


def project(pieces, w_own, w_other, cos, sin, first, steps, turns):
    n = sum(x.shape[0] for x in pieces)
    width, cols = w_own.shape[1:]
    whole = lambda x: pl.BlockSpec(x.shape, lambda i: (0, 0))
    return pl.pallas_call(
        functools.partial(project_kernel, turns),
        grid=(steps,),
        in_specs=[whole(x) for x in pieces]
        + [pl.BlockSpec((1, width, cols), lambda i: (first + i, 0, 0))] * 2
        + [whole(cos), whole(sin)],
        out_specs=pl.BlockSpec((n, 2 * cols), lambda i: (0, i)),
        out_shape=jax.ShapeDtypeStruct((n, 2 * cols * steps), bf16),
        scratch_shapes=[pltpu.VMEM((n, width), bf16)],
        compiler_params=pltpu.CompilerParams(vmem_limit_bytes=48 * MIB),
        cost_estimate=pl.CostEstimate(
            flops=4 * steps * n * width * cols, bytes_accessed=2 * width * (n + 2 * steps * cols), transcendentals=0
        ),
        name="project",
    )(*pieces, w_own, w_other, cos, sin)


def attend_kernel(at, sizes, q, kv_own, kv_got, pos_q, pos_own, pos_got, w_own, w_other, *refs):
    *outs, near, w, sems = refs
    n = sum(sizes)
    heads = q.shape[1] // HD
    half = heads * HD
    cols = w_own.shape[0]
    routes = [
        (kv_own.at[:, :half], near.at[0]),
        (kv_got.at[:, :half], near.at[1]),
        (kv_own.at[:, half:], near.at[2]),
        (kv_got.at[:, half:], near.at[3]),
        (w_own, w.at[:cols, :]),
        (w_other, w.at[cols:, :]),
    ]
    copies = [pltpu.make_async_copy(a, b, sems.at[i]) for i, (a, b) in enumerate(routes)]
    for copy in copies:
        copy.start()
    rows_at = pos_q[at : at + n, :]
    seen_own = pos_own[...] <= rows_at
    seen_got = pos_got[...] <= rows_at
    scale = HD ** (-0.5)
    contract = (((1,), (1,)), ((), ()))
    copies[0].wait()
    copies[1].wait()
    mixed = []
    for h in range(heads):
        g = (h + heads // 2) % heads
        mine, its = slice(h * HD, (h + 1) * HD), slice(g * HD, (g + 1) * HD)
        qh = q[at : at + n, mine]
        s_own = lax.dot_general(qh, near[0, :, mine], contract, preferred_element_type=f32) * scale
        s_got = lax.dot_general(qh, near[1, :, its], contract, preferred_element_type=f32) * scale
        s_own = jnp.where(seen_own, s_own, -1e30)
        s_got = jnp.where(seen_got, s_got, -1e30)
        top = jnp.maximum(jnp.max(s_own, axis=-1, keepdims=True), jnp.max(s_got, axis=-1, keepdims=True))
        e_own = jnp.exp(s_own - top)
        e_got = jnp.exp(s_got - top)
        inverse = 1.0 / (jnp.sum(e_own, axis=-1, keepdims=True) + jnp.sum(e_got, axis=-1, keepdims=True))
        if h == 0:
            copies[2].wait()
            copies[3].wait()
        o = dot((e_own * inverse).astype(bf16), near[2, :, mine]) + dot((e_got * inverse).astype(bf16), near[3, :, its])
        mixed.append(o.astype(bf16))
    copies[4].wait()
    copies[5].wait()
    total = dot(jnp.concatenate(mixed, axis=1), w[...]).astype(bf16)
    start = 0
    for out, size in zip(outs, sizes):
        out[...] = total[start : start + size]
        start += size


def attend(at, sizes, q, kv_own, kv_got, pos_q, pos_own, pos_got, w_own, w_other):
    cols, width = w_own.shape
    rows = kv_own.shape[0]
    n = sum(sizes)
    heads = q.shape[1] // HD
    near, anywhere = pl.BlockSpec(memory_space=pltpu.VMEM), pl.BlockSpec(memory_space=pl.ANY)
    return pl.pallas_call(
        functools.partial(attend_kernel, at, sizes),
        in_specs=[near, anywhere, anywhere, near, near, near, anywhere, anywhere],
        out_specs=[near] * len(sizes),
        out_shape=[jax.ShapeDtypeStruct((size, width), bf16) for size in sizes],
        scratch_shapes=[
            pltpu.VMEM((4, rows, heads * HD), bf16),
            pltpu.VMEM((2 * cols, width), bf16),
            pltpu.SemaphoreType.DMA((6,)),
        ],
        compiler_params=pltpu.CompilerParams(vmem_limit_bytes=28 * MIB),
        cost_estimate=pl.CostEstimate(
            flops=16 * n * rows * heads * HD + 2 * n * heads * HD * width,
            bytes_accessed=2 * (q.size + 2 * kv_own.size + 2 * w_own.size + n * width),
            transcendentals=2 * n * rows * heads,
        ),
        name="attend",
    )(q, kv_own, kv_got, pos_q, pos_own, pos_got, w_own, w_other)


def expert_kernel(count, parts, sides, added, *refs):
    take = lambda n: (refs[:n], refs[n:])
    pieces, refs = take(count)
    gate_ups, refs = take(sides)
    down_projs, refs = take(sides)
    bases, refs = take(parts * added)
    outs, (x, gates, downs, hidden, gate_sems, down_sems) = take(parts)
    tile = gates.shape[3]
    tiles = gate_ups[0].shape[2] // tile
    steps = sides * tiles
    slots = gates.shape[0]
    mid = down_projs[0].shape[0]

    def fetch(i):
        side, slot = i // tiles, i % slots
        for number, source in enumerate(gate_ups):

            @pl.when(side == number)
            def _():
                part = source.at[:, :, pl.ds((i % tiles) * tile, tile)]
                pltpu.make_async_copy(part, gates.at[slot], gate_sems.at[slot]).start()

    for i in range(slots - 1):
        fetch(i)
    at = 0
    for piece in pieces:
        x[at : at + piece.shape[0], :] = piece[...]
        at += piece.shape[0]
    to_down = [
        pltpu.make_async_copy(source, downs.at[pl.ds(number * mid, mid), :], down_sems.at[number])
        for number, source in enumerate(down_projs)
    ]

    def step(i, carry):
        slot = i % slots

        @pl.when(i + slots - 1 < steps)
        def _():
            fetch(i + slots - 1)

        for number in range(sides):

            @pl.when(i == (tiles * number if number else min(1, steps - 1)))
            def _():
                to_down[number].start()

        pltpu.make_async_copy(gate_ups[0].at[:, :, pl.ds(0, tile)], gates.at[slot], gate_sems.at[slot]).wait()
        rows = x[...]
        g = dot(rows, gates[slot, 0])
        u = dot(rows, gates[slot, 1])
        hidden[i] = (g / (1.0 + jnp.exp(-g)) * u).astype(bf16)
        return carry

    lax.fori_loop(0, steps, step, 0)
    for copy in to_down:
        copy.wait()
    rows = jnp.concatenate([hidden[i] for i in range(steps)], axis=1)
    width = x.shape[1]
    for left in range(0, width, width // 4):
        cols = slice(left, left + width // 4)
        part = dot(rows, downs[:, cols])
        at = 0
        for j, out in enumerate(outs):
            mine = part[at : at + out.shape[0]]
            if added:
                mine = mine + bases[j][:, cols].astype(f32)
            out[:, cols] = mine.astype(bf16)
            at += out.shape[0]


def expert(pieces, sizes, gate_ups, down_projs, bases=()):
    n, width = sum(x.shape[0] for x in pieces), pieces[0].shape[1]
    mid = down_projs[0].shape[0]
    sides = len(gate_ups)
    tile = 256 if mid % 256 == 0 else mid
    slots = 3
    anywhere = pl.BlockSpec(memory_space=pl.ANY)
    near = pl.BlockSpec(memory_space=pltpu.VMEM)
    return pl.pallas_call(
        functools.partial(expert_kernel, len(pieces), len(sizes), sides, int(bool(bases))),
        in_specs=[near] * len(pieces) + [anywhere] * (2 * sides) + [near] * len(bases),
        out_specs=[near] * len(sizes),
        out_shape=[jax.ShapeDtypeStruct((size, width), bf16) for size in sizes],
        scratch_shapes=[
            pltpu.VMEM((n, width), bf16),
            pltpu.VMEM((slots, 2, width, tile), bf16),
            pltpu.VMEM((sides * mid, width), bf16),
            pltpu.VMEM((sides * mid // tile, n, tile), bf16),
            pltpu.SemaphoreType.DMA((slots,)),
            pltpu.SemaphoreType.DMA((sides,)),
        ],
        compiler_params=pltpu.CompilerParams(vmem_limit_bytes=44 * MIB),
        cost_estimate=pl.CostEstimate(
            flops=6 * sides * n * width * mid,
            bytes_accessed=2 * (2 * n * width + 3 * sides * width * mid),
            transcendentals=sides * n * mid,
        ),
        name="experts",
    )(*pieces, *gate_ups, *down_projs, *bases)


def body(tokens, expert_ids, slot_ids, norm_attn, w_qkv, w_out, norm_moe, router_weight, w_gate_up, w_down):
    rows = tokens.shape[1]
    width = tokens.shape[2]
    cols = w_qkv.shape[2]
    y, xl, core = lax.axis_index("y"), lax.axis_index("xl"), lax.axis_index("core")

    normed = small(norm_kernel, "norm", like(rows, tokens[0]), tokens[0], norm_attn[None])

    def place(group):
        rows_of = []
        for dy, dx, at, n in group:
            start = (((y + dy) % 4) * 4 + (xl ^ dx) * 2) * rows + at * (rows // 4)
            rows_of.append(start + jnp.arange(n * (rows // 4), dtype=jnp.int32))
        return cat(*rows_of)

    wq_own = w_qkv.transpose(1, 0, 2)
    base = cat(*[place(g) for g in origins()])
    pos_own = base + core * rows
    pos_got = base + (1 - core) * rows
    experts = router_weight.shape[1]
    capacity = 3 * rows // experts // 2
    cells = jnp.where(slot_ids[0] < capacity, expert_ids[0] * capacity + slot_ids[0], -1)
    tables = (*rope_tables(pos_own), pos_own[:, None], pos_own[None], pos_got[None])
    one, (wq_own, gate_up, *tables) = gather_one(normed, wq_own, w_gate_up, *tables)
    cos, sin, *places = tables
    wq_other = to_core(wq_own)
    wo_other = to_core(w_out)
    wgu_own = gate_up[0].transpose(1, 0, 2)
    two, (wgu_own, wq_other, wo_other) = gather_two(one, wgu_own, wq_other, wo_other)
    three, _ = gather_three(two)

    one = one[:3]
    pieces = (*one, *two, *three)
    kv_own = project(pieces, wq_own, wq_other, cos, sin, 1, 2, 1)
    kv_got = to_core(kv_own)
    q_all = project(pieces, wq_own, wq_other, cos, sin, 0, 1, 1)
    kv_got, q_all, wgu_own, wd_own = tie(kv_got, q_all, wgu_own, w_down[0])
    wgu_other = to_core(wgu_own)
    wd_other = to_core(wd_own)
    sizes = [merged(one, 1), tuple(x.shape[0] for x in two), tuple(x.shape[0] for x in three)]

    def attended(group):
        at = sum(sum(before) for before in sizes[:group])
        return attend(
            at, sizes[group], q_all, kv_own, kv_got, *places, w_out, wo_other
        )

    got = scatter_three(attended(2))
    got = scatter_two(attended(1), got)
    attn_terms, (wgu_other, wd_other) = scatter_one(attended(0), got, wgu_other, wd_other)

    blocks = jax.ShapeDtypeStruct((experts, capacity * width // HD, HD), bf16)
    residual, weight_one, weight_two, outgoing = small(
        functools.partial(route_kernel, capacity),
        "route",
        [like(rows, tokens[0])] + [jax.ShapeDtypeStruct((rows, 1), f32)] * 2 + [blocks],
        tokens[0],
        *attn_terms,
        norm_moe[None],
        router_weight,
        expert_ids[0],
        cells.T,
    )
    packed = like(experts * capacity, tokens[0])
    arrived = small(functools.partial(unpack_kernel, capacity), "unpack", packed, exchange(outgoing))

    both = (wgu_own, wgu_other), (wd_own, wd_other)
    one, _ = gather_one(arrived)
    two, part_one = gather_two(one, *expert(one[:3], merged(one[:3], 1), *both))
    size_two = tuple(x.shape[0] for x in two)
    three, base = gather_three(two, *expert(two, size_two, (wgu_own,), (wd_own,)))
    got = scatter_three(expert(three, tuple(x.shape[0] for x in three), *both))
    got = scatter_two(expert(two, size_two, (wgu_other,), (wd_other,), base), got)
    expert_terms, _ = scatter_one(part_one, got)
    finished = small(functools.partial(pack_kernel, capacity), "pack", blocks, *expert_terms)
    returned = exchange(finished)
    out = small(
        functools.partial(combine_kernel, capacity),
        "combine",
        like(rows, tokens[0]),
        residual,
        weight_one,
        weight_two,
        cells,
        returned,
    )
    return out[None]


def solution(mesh):
    names = ("z", "xh", "y", "xl", "core")
    split = Mesh(mesh.devices.reshape(4, 2, 4, 2, 2), names)
    expert = ("z", "xh")
    tensor = ("y", "xl", "core")
    placed = (
        P(expert, tensor, None),
        P(expert, tensor, None),
        P(expert, tensor, None),
        P(),
        P(None, None, tensor),
        P(tensor, None),
        P(),
        P(),
        P(expert, None, None, tensor),
        P(expert, tensor, None),
    )
    return jax.shard_map(body, mesh=split, in_specs=placed, out_specs=P(expert, tensor, None), check_vma=False)
```

```python
import functools

import jax
import jax.numpy as jnp
from jax import lax
from jax.experimental import pallas as pl
from jax.experimental.pallas import tpu as pltpu
from jax.sharding import Mesh
from jax.sharding import PartitionSpec as P

HD = 128
EPS = 1e-05
NEXT_Y = [(i, (i + 1) % 4) for i in range(4)]
PREV_Y = [(i, (i + 3) % 4) for i in range(4)]
PAIR = [(0, 1), (1, 0)]

bf16 = jnp.bfloat16
f32 = jnp.float32
MIB = 1024 * 1024


def to_next(v):
    return lax.ppermute(v, "y", NEXT_Y)


def to_prev(v):
    return lax.ppermute(v, "y", PREV_Y)


def to_side(v):
    return lax.ppermute(v, "xl", PAIR)


def to_core(v):
    return lax.ppermute(v, "core", PAIR)


def cat(*parts):
    return jnp.concatenate(parts, axis=0)


def tie(*values):
    return lax.optimization_barrier(values)


def split(x, *parts):
    out, at = [], 0
    for n in parts:
        out.append(x[at : at + n])
        at += n
    return out


def cut(h):
    return h // 2 // 16 * 16


def gather_one(x, *beside):
    h = x.shape[0] // 2
    a, b = x[:h], x[h:]
    a_side, b_m, b_p, *beside = tie(to_side(a), to_next(b), to_prev(b), *beside)
    return (cat(a, a_side), b, cat(b_m, b_p), to_side(b)), beside


def gather_two(one, *beside):
    aa, _, b_mp, b_side = one
    h = aa.shape[0] // 2
    q = cut(h)
    up = cat(aa, b_mp[:q])
    down = cat(aa, b_mp[h + q :])
    m, p, b_side, side, *beside = tie(to_next(up), to_prev(down), b_side, to_side(b_mp), *beside)
    return (m, p, b_side, side), beside


def gather_three(two, *beside):
    m, p, side, _ = two
    h = side.shape[0]
    far_a, far_b, far_c, *beside = tie(
        to_next(m[:h]), to_prev(p[h : 2 * h]), to_side(cat(m[2 * h :], p[2 * h :])), *beside
    )
    return (far_a, far_b, far_c), beside


def merged(pieces, at):
    sizes = [x.shape[0] for x in pieces]
    return (*sizes[:at], sum(sizes[at:]))


def origins():
    one = [(0, 0, 0, 2), (0, 1, 0, 2), (0, 0, 2, 2), (3, 0, 2, 2), (1, 0, 2, 2)]
    two = [(3, 0, 0, 2), (3, 1, 0, 2), (2, 0, 2, 1), (1, 0, 0, 2), (1, 1, 0, 2), (2, 0, 3, 1)]
    two += [(0, 1, 2, 2), (3, 1, 2, 2), (1, 1, 2, 2)]
    three = [(2, 0, 0, 2), (2, 1, 0, 2), (2, 1, 2, 2)]
    return one, two, three


def small(kernel, name, outs, *args):
    size = sum(x.size * x.dtype.itemsize for x in (*args, *jax.tree.leaves(outs)))
    return pl.pallas_call(
        kernel,
        out_shape=outs,
        compiler_params=pltpu.CompilerParams(vmem_limit_bytes=28 * MIB),
        cost_estimate=pl.CostEstimate(flops=size, bytes_accessed=size, transcendentals=0),
        name=name,
    )(*args)


def like(rows, x, dtype=bf16):
    return jax.ShapeDtypeStruct((rows, x.shape[1]), dtype)


def scatter_three(three):
    a, b, c = three
    return tie(to_prev(a), to_next(b), to_side(c))


def add_far(h, q, m, p, g_a, g_b, g_c, m_out, p_out):
    plus = lambda a, b: (a.astype(f32) + b.astype(f32)).astype(bf16)
    m_out[:h] = plus(m[:h], g_a[...])
    m_out[h : 2 * h] = m[h : 2 * h]
    m_out[2 * h :] = plus(m[2 * h :], g_c[:q])
    p_out[:h] = p[:h]
    p_out[h : 2 * h] = plus(p[h : 2 * h], g_b[...])
    p_out[2 * h :] = plus(p[2 * h :], g_c[q:])


def scatter_two(two, got):
    m, p, b_side, side = two
    h = b_side.shape[0]
    m, p = small(functools.partial(add_far, h, cut(h)), "add_far", [like(m.shape[0], m), like(p.shape[0], p)], m, p, *got)
    return (*tie(to_prev(m), to_next(p), to_side(side)), to_side(b_side))


def add_near(h, q, aa, bb, g_m, g_p, g_side, a_out, m_out, p_out, a_keep, b_keep):
    plus = lambda *terms: functools.reduce(jnp.add, [t.astype(f32) for t in terms])
    a_keep[...] = plus(aa[:h], g_m[:h], g_p[:h])
    a_out[...] = plus(aa[h:], g_m[h : 2 * h], g_p[h : 2 * h]).astype(bf16)
    b_keep[...] = bb[:h].astype(f32)
    m_out[:q] = plus(bb[h : h + q], g_side[:q], g_m[2 * h :]).astype(bf16)
    m_out[q:] = plus(bb[h + q : 2 * h], g_side[q:h]).astype(bf16)
    p_out[:q] = plus(bb[2 * h : 2 * h + q], g_side[h : h + q]).astype(bf16)
    p_out[q:] = plus(bb[2 * h + q :], g_side[h + q :], g_p[2 * h :]).astype(bf16)


def scatter_one(one, got, *beside):
    aa, bb = one
    h = aa.shape[0] // 2
    outs = [like(h, aa)] * 3 + [like(h, aa, f32)] * 2
    a, m, p, a_keep, b_keep = small(functools.partial(add_near, h, cut(h)), "add_near", outs, aa, bb, *got[:3])
    l_a, l_b, l_m, l_p, *beside = tie(to_side(a), got[3], to_prev(m), to_next(p), *beside)
    return (a_keep, l_a, b_keep, l_b, l_m, l_p), beside


def total_of(a_keep, l_a, b_keep, l_b, l_m, l_p):
    top = a_keep[...] + l_a[...].astype(f32)
    low = b_keep[...] + l_b[...].astype(f32) + l_m[...].astype(f32) + l_p[...].astype(f32)
    return jnp.concatenate([top, low], axis=0)


def exchange(blocks):
    return lax.all_to_all(blocks, ("z", "xh"), split_axis=0, concat_axis=0, tiled=True)


def columns(g, i):
    return slice((4 * g + i) * HD, (4 * g + i + 1) * HD)


def lines(g, capacity):
    return slice(4 * capacity * g, 4 * capacity * (g + 1))


def one_hot(hit):
    return jnp.where(hit, 1.0, 0.0).astype(bf16)


def line_parts(shape, dim, capacity):
    line = lax.broadcasted_iota(jnp.int32, shape, dim)
    rest = line % (4 * capacity)
    return line // (4 * capacity) * capacity + rest % capacity, rest // capacity


def to_lines(capacity, rows, choose, out):
    for g in range(rows.shape[1] // (4 * HD)):
        stack = jnp.concatenate([rows[:, columns(g, i)] for i in range(4)], axis=0)
        done = dot(choose, stack).astype(bf16)
        for k in range(out.shape[0]):
            out[k, lines(g, capacity), :] = done[4 * capacity * k : 4 * capacity * (k + 1)]


def line_stack(blocks, g, capacity):
    return jnp.concatenate([blocks[k, lines(g, capacity), :] for k in range(blocks.shape[0])], axis=0)


def route_kernel(capacity, tok, a_keep, l_a, b_keep, l_b, l_m, l_p, gain, router, ids, cells, res, one, two, out):
    residual = (tok[...].astype(f32) + total_of(a_keep, l_a, b_keep, l_b, l_m, l_p)).astype(bf16)
    res[...] = residual
    values = residual.astype(f32)
    scale = lax.rsqrt(jnp.mean(values * values, axis=-1, keepdims=True) + EPS)
    normed = (values * scale * gain[...].astype(f32)).astype(bf16)
    logits = dot(normed, router[...])
    label = lax.broadcasted_iota(jnp.int32, logits.shape, 1)
    first = jnp.sum(jnp.where(label == ids[:, 0:1], logits, 0.0), axis=-1, keepdims=True)
    second = jnp.sum(jnp.where(label == ids[:, 1:2], logits, 0.0), axis=-1, keepdims=True)
    one[...] = 1.0 / (1.0 + jnp.exp(second - first))
    two[...] = 1.0 / (1.0 + jnp.exp(first - second))
    rows = tok.shape[0]
    slot, part = line_parts((4 * capacity * out.shape[0], rows), 0, capacity)
    hit = (slot == cells[0:1, :]) | (slot == cells[1:2, :])
    to_lines(capacity, normed, jnp.concatenate([one_hot(hit & (part == i)) for i in range(4)], axis=1), out)


def unpack_kernel(capacity, blocks, out):
    shape = (out.shape[0], 4 * capacity * blocks.shape[0])
    row = lax.broadcasted_iota(jnp.int32, shape, 0)
    slot, part = line_parts(shape, 1, capacity)
    choose = [one_hot((slot == row) & (part == i)) for i in range(4)]
    for g in range(out.shape[1] // (4 * HD)):
        stack = line_stack(blocks, g, capacity)
        for i in range(4):
            out[:, columns(g, i)] = dot(choose[i], stack).astype(bf16)


def pack_kernel(capacity, a_keep, l_a, b_keep, l_b, l_m, l_p, out):
    total = total_of(a_keep, l_a, b_keep, l_b, l_m, l_p).astype(bf16)
    shape = (4 * capacity * out.shape[0], total.shape[0])
    row = lax.broadcasted_iota(jnp.int32, shape, 1)
    slot, part = line_parts(shape, 0, capacity)
    choose = jnp.concatenate([one_hot((slot == row) & (part == i)) for i in range(4)], axis=1)
    to_lines(capacity, total, choose, out)


def combine_kernel(capacity, res, one, two, cells, blocks, out):
    slot, part = line_parts((res.shape[0], 4 * capacity * blocks.shape[0]), 1, capacity)
    first = [one_hot((slot == cells[:, 0:1]) & (part == i)) for i in range(4)]
    second = [one_hot((slot == cells[:, 1:2]) & (part == i)) for i in range(4)]
    for g in range(out.shape[1] // (4 * HD)):
        stack = line_stack(blocks, g, capacity)
        for i in range(4):
            mix = one[...] * dot(first[i], stack) + two[...] * dot(second[i], stack)
            out[:, columns(g, i)] = (res[:, columns(g, i)].astype(f32) + mix).astype(bf16)


def norm_kernel(tok, gain, out):
    values = tok[...].astype(f32)
    scale = lax.rsqrt(jnp.mean(values * values, axis=-1, keepdims=True) + EPS)
    out[...] = (values * scale * gain[...].astype(f32)).astype(bf16)


def rope_tables(positions):
    half = HD // 2
    frequencies = jnp.exp(-jnp.log(10000.0) * jnp.arange(half, dtype=f32) / half)
    angles = positions.astype(f32)[:, None] * frequencies[None, :]
    cosine, sine = jnp.cos(angles), jnp.sin(angles)
    return jnp.concatenate([cosine, cosine], axis=1), jnp.concatenate([-sine, sine], axis=1)


def dot(a, b):
    return jnp.dot(a, b, preferred_element_type=f32)


def project_kernel(turns, *refs):
    *pieces, w_own, w_other, cos, sin, out, rows = refs
    step = pl.program_id(0)
    cols = w_own.shape[2]

    @pl.when(step == 0)
    def _():
        at = 0
        for x in pieces:
            rows[at : at + x.shape[0], :] = x[...]
            at += x.shape[0]

    turned = step < turns
    c = jnp.where(turned, cos[...], 1.0)
    s = jnp.where(turned, sin[...], 0.0)
    done = []
    for w in (w_own, w_other):
        acc = dot(rows[...], w[0])
        for j in range(cols // HD):
            part = acc[:, j * HD : (j + 1) * HD]
            done.append((part * c + pltpu.roll(part, HD // 2, 1) * s).astype(bf16))
    out[...] = jnp.concatenate(done, axis=1)


def project(pieces, w_own, w_other, cos, sin, first, steps, turns):
    n = sum(x.shape[0] for x in pieces)
    width, cols = w_own.shape[1:]
    whole = lambda x: pl.BlockSpec(x.shape, lambda i: (0, 0))
    return pl.pallas_call(
        functools.partial(project_kernel, turns),
        grid=(steps,),
        in_specs=[whole(x) for x in pieces]
        + [pl.BlockSpec((1, width, cols), lambda i: (first + i, 0, 0))] * 2
        + [whole(cos), whole(sin)],
        out_specs=pl.BlockSpec((n, 2 * cols), lambda i: (0, i)),
        out_shape=jax.ShapeDtypeStruct((n, 2 * cols * steps), bf16),
        scratch_shapes=[pltpu.VMEM((n, width), bf16)],
        compiler_params=pltpu.CompilerParams(vmem_limit_bytes=48 * MIB),
        cost_estimate=pl.CostEstimate(
            flops=4 * steps * n * width * cols, bytes_accessed=2 * width * (n + 2 * steps * cols), transcendentals=0
        ),
        name="project",
    )(*pieces, w_own, w_other, cos, sin)


def attend_kernel(at, sizes, q, kv_own, kv_got, pos_q, pos_own, pos_got, w_own, w_other, *refs):
    *outs, near, w, sems = refs
    n = sum(sizes)
    heads = q.shape[1] // HD
    half = heads * HD
    cols = w_own.shape[0]
    routes = [
        (kv_own.at[:, :half], near.at[0]),
        (kv_got.at[:, :half], near.at[1]),
        (kv_own.at[:, half:], near.at[2]),
        (kv_got.at[:, half:], near.at[3]),
        (w_own, w.at[:cols, :]),
        (w_other, w.at[cols:, :]),
    ]
    copies = [pltpu.make_async_copy(a, b, sems.at[i]) for i, (a, b) in enumerate(routes)]
    for copy in copies:
        copy.start()
    rows_at = pos_q[at : at + n, :]
    seen_own = pos_own[...] <= rows_at
    seen_got = pos_got[...] <= rows_at
    scale = HD ** (-0.5)
    contract = (((1,), (1,)), ((), ()))
    copies[0].wait()
    copies[1].wait()
    mixed = []
    for h in range(heads):
        g = (h + heads // 2) % heads
        mine, its = slice(h * HD, (h + 1) * HD), slice(g * HD, (g + 1) * HD)
        qh = q[at : at + n, mine]
        s_own = lax.dot_general(qh, near[0, :, mine], contract, preferred_element_type=f32) * scale
        s_got = lax.dot_general(qh, near[1, :, its], contract, preferred_element_type=f32) * scale
        s_own = jnp.where(seen_own, s_own, -1e30)
        s_got = jnp.where(seen_got, s_got, -1e30)
        top = jnp.maximum(jnp.max(s_own, axis=-1, keepdims=True), jnp.max(s_got, axis=-1, keepdims=True))
        e_own = jnp.exp(s_own - top)
        e_got = jnp.exp(s_got - top)
        inverse = 1.0 / (jnp.sum(e_own, axis=-1, keepdims=True) + jnp.sum(e_got, axis=-1, keepdims=True))
        if h == 0:
            copies[2].wait()
            copies[3].wait()
        o = dot((e_own * inverse).astype(bf16), near[2, :, mine]) + dot((e_got * inverse).astype(bf16), near[3, :, its])
        mixed.append(o.astype(bf16))
    copies[4].wait()
    copies[5].wait()
    total = dot(jnp.concatenate(mixed, axis=1), w[...]).astype(bf16)
    start = 0
    for out, size in zip(outs, sizes):
        out[...] = total[start : start + size]
        start += size


def attend(at, sizes, q, kv_own, kv_got, pos_q, pos_own, pos_got, w_own, w_other):
    cols, width = w_own.shape
    rows = kv_own.shape[0]
    n = sum(sizes)
    heads = q.shape[1] // HD
    near, anywhere = pl.BlockSpec(memory_space=pltpu.VMEM), pl.BlockSpec(memory_space=pl.ANY)
    return pl.pallas_call(
        functools.partial(attend_kernel, at, sizes),
        in_specs=[near, anywhere, anywhere, near, near, near, anywhere, anywhere],
        out_specs=[near] * len(sizes),
        out_shape=[jax.ShapeDtypeStruct((size, width), bf16) for size in sizes],
        scratch_shapes=[
            pltpu.VMEM((4, rows, heads * HD), bf16),
            pltpu.VMEM((2 * cols, width), bf16),
            pltpu.SemaphoreType.DMA((6,)),
        ],
        compiler_params=pltpu.CompilerParams(vmem_limit_bytes=28 * MIB),
        cost_estimate=pl.CostEstimate(
            flops=16 * n * rows * heads * HD + 2 * n * heads * HD * width,
            bytes_accessed=2 * (q.size + 2 * kv_own.size + 2 * w_own.size + n * width),
            transcendentals=2 * n * rows * heads,
        ),
        name="attend",
    )(q, kv_own, kv_got, pos_q, pos_own, pos_got, w_own, w_other)


def expert_kernel(count, parts, sides, added, *refs):
    take = lambda n: (refs[:n], refs[n:])
    pieces, refs = take(count)
    gate_ups, refs = take(sides)
    down_projs, refs = take(sides)
    bases, refs = take(parts * added)
    outs, (x, gates, downs, hidden, gate_sems, down_sems) = take(parts)
    tile = gates.shape[3]
    tiles = gate_ups[0].shape[2] // tile
    steps = sides * tiles
    slots = gates.shape[0]
    mid = down_projs[0].shape[0]

    def fetch(i):
        side, slot = i // tiles, i % slots
        for number, source in enumerate(gate_ups):

            @pl.when(side == number)
            def _():
                part = source.at[:, :, pl.ds((i % tiles) * tile, tile)]
                pltpu.make_async_copy(part, gates.at[slot], gate_sems.at[slot]).start()

    for i in range(slots - 1):
        fetch(i)
    at = 0
    for piece in pieces:
        x[at : at + piece.shape[0], :] = piece[...]
        at += piece.shape[0]
    to_down = [
        pltpu.make_async_copy(source, downs.at[pl.ds(number * mid, mid), :], down_sems.at[number])
        for number, source in enumerate(down_projs)
    ]

    def step(i, carry):
        slot = i % slots

        @pl.when(i + slots - 1 < steps)
        def _():
            fetch(i + slots - 1)

        for number in range(sides):

            @pl.when(i == (tiles * number if number else min(1, steps - 1)))
            def _():
                to_down[number].start()

        pltpu.make_async_copy(gate_ups[0].at[:, :, pl.ds(0, tile)], gates.at[slot], gate_sems.at[slot]).wait()
        rows = x[...]
        g = dot(rows, gates[slot, 0])
        u = dot(rows, gates[slot, 1])
        hidden[i] = (g / (1.0 + jnp.exp(-g)) * u).astype(bf16)
        return carry

    lax.fori_loop(0, steps, step, 0)
    for copy in to_down:
        copy.wait()
    rows = jnp.concatenate([hidden[i] for i in range(steps)], axis=1)
    width = x.shape[1]
    for left in range(0, width, width // 4):
        cols = slice(left, left + width // 4)
        part = dot(rows, downs[:, cols])
        at = 0
        for j, out in enumerate(outs):
            mine = part[at : at + out.shape[0]]
            if added:
                mine = mine + bases[j][:, cols].astype(f32)
            out[:, cols] = mine.astype(bf16)
            at += out.shape[0]


def expert(pieces, sizes, gate_ups, down_projs, bases=()):
    n, width = sum(x.shape[0] for x in pieces), pieces[0].shape[1]
    mid = down_projs[0].shape[0]
    sides = len(gate_ups)
    tile = 256 if mid % 256 == 0 else mid
    slots = 4
    anywhere = pl.BlockSpec(memory_space=pl.ANY)
    near = pl.BlockSpec(memory_space=pltpu.VMEM)
    return pl.pallas_call(
        functools.partial(expert_kernel, len(pieces), len(sizes), sides, int(bool(bases))),
        in_specs=[near] * len(pieces) + [anywhere] * (2 * sides) + [near] * len(bases),
        out_specs=[near] * len(sizes),
        out_shape=[jax.ShapeDtypeStruct((size, width), bf16) for size in sizes],
        scratch_shapes=[
            pltpu.VMEM((n, width), bf16),
            pltpu.VMEM((slots, 2, width, tile), bf16),
            pltpu.VMEM((sides * mid, width), bf16),
            pltpu.VMEM((sides * mid // tile, n, tile), bf16),
            pltpu.SemaphoreType.DMA((slots,)),
            pltpu.SemaphoreType.DMA((sides,)),
        ],
        compiler_params=pltpu.CompilerParams(vmem_limit_bytes=44 * MIB),
        cost_estimate=pl.CostEstimate(
            flops=6 * sides * n * width * mid,
            bytes_accessed=2 * (2 * n * width + 3 * sides * width * mid),
            transcendentals=sides * n * mid,
        ),
        name="experts",
    )(*pieces, *gate_ups, *down_projs, *bases)


def body(tokens, expert_ids, slot_ids, norm_attn, w_qkv, w_out, norm_moe, router_weight, w_gate_up, w_down):
    rows = tokens.shape[1]
    width = tokens.shape[2]
    cols = w_qkv.shape[2]
    y, xl, core = lax.axis_index("y"), lax.axis_index("xl"), lax.axis_index("core")

    normed = small(norm_kernel, "norm", like(rows, tokens[0]), tokens[0], norm_attn[None])

    def place(group):
        rows_of = []
        for dy, dx, at, n in group:
            start = (((y + dy) % 4) * 4 + (xl ^ dx) * 2) * rows + at * (rows // 4)
            rows_of.append(start + jnp.arange(n * (rows // 4), dtype=jnp.int32))
        return cat(*rows_of)

    wq_own = w_qkv.transpose(1, 0, 2)
    base = cat(*[place(g) for g in origins()])
    pos_own = base + core * rows
    pos_got = base + (1 - core) * rows
    experts = router_weight.shape[1]
    capacity = 3 * rows // experts // 2
    cells = jnp.where(slot_ids[0] < capacity, expert_ids[0] * capacity + slot_ids[0], -1)
    tables = (*rope_tables(pos_own), pos_own[:, None], pos_own[None], pos_got[None])
    one, (wq_own, gate_up, *tables) = gather_one(normed, wq_own, w_gate_up, *tables)
    cos, sin, *places = tables
    wq_other = to_core(wq_own)
    wo_other = to_core(w_out)
    wgu_own = gate_up[0].transpose(1, 0, 2)
    two, (wgu_own, wq_other, wo_other) = gather_two(one, wgu_own, wq_other, wo_other)
    three, _ = gather_three(two)

    one = one[:3]
    pieces = (*one, *two, *three)
    kv_own = project(pieces, wq_own, wq_other, cos, sin, 1, 2, 1)
    kv_got = to_core(kv_own)
    q_all = project(pieces, wq_own, wq_other, cos, sin, 0, 1, 1)
    kv_got, q_all, wgu_own, wd_own = tie(kv_got, q_all, wgu_own, w_down[0])
    wgu_other = to_core(wgu_own)
    wd_other = to_core(wd_own)
    sizes = [merged(one, 1), tuple(x.shape[0] for x in two), tuple(x.shape[0] for x in three)]

    def attended(group):
        at = sum(sum(before) for before in sizes[:group])
        return attend(
            at, sizes[group], q_all, kv_own, kv_got, *places, w_out, wo_other
        )

    got = scatter_three(attended(2))
    got = scatter_two(attended(1), got)
    attn_terms, (wgu_other, wd_other) = scatter_one(attended(0), got, wgu_other, wd_other)

    blocks = jax.ShapeDtypeStruct((experts, capacity * width // HD, HD), bf16)
    residual, weight_one, weight_two, outgoing = small(
        functools.partial(route_kernel, capacity),
        "route",
        [like(rows, tokens[0])] + [jax.ShapeDtypeStruct((rows, 1), f32)] * 2 + [blocks],
        tokens[0],
        *attn_terms,
        norm_moe[None],
        router_weight,
        expert_ids[0],
        cells.T,
    )
    packed = like(experts * capacity, tokens[0])
    arrived = small(functools.partial(unpack_kernel, capacity), "unpack", packed, exchange(outgoing))

    both = (wgu_own, wgu_other), (wd_own, wd_other)
    one, _ = gather_one(arrived)
    two, part_one = gather_two(one, *expert(one[:3], merged(one[:3], 1), *both))
    size_two = tuple(x.shape[0] for x in two)
    three, base = gather_three(two, *expert(two, size_two, (wgu_own,), (wd_own,)))
    got = scatter_three(expert(three, tuple(x.shape[0] for x in three), *both))
    got = scatter_two(expert(two, size_two, (wgu_other,), (wd_other,), base), got)
    expert_terms, _ = scatter_one(part_one, got)
    finished = small(functools.partial(pack_kernel, capacity), "pack", blocks, *expert_terms)
    returned = exchange(finished)
    out = small(
        functools.partial(combine_kernel, capacity),
        "combine",
        like(rows, tokens[0]),
        residual,
        weight_one,
        weight_two,
        cells,
        returned,
    )
    return out[None]


def solution(mesh):
    names = ("z", "xh", "y", "xl", "core")
    split = Mesh(mesh.devices.reshape(4, 2, 4, 2, 2), names)
    expert = ("z", "xh")
    tensor = ("y", "xl", "core")
    placed = (
        P(expert, tensor, None),
        P(expert, tensor, None),
        P(expert, tensor, None),
        P(),
        P(None, None, tensor),
        P(tensor, None),
        P(),
        P(),
        P(expert, None, None, tensor),
        P(expert, tensor, None),
    )
    return jax.shard_map(body, mesh=split, in_specs=placed, out_specs=P(expert, tensor, None), check_vma=False)
```
